256 devices in a mesh: grp: 8 (over x, core), dev: 32 (over y, z).
Axes of the slice: x: 4, y: 4, z: 8, core: 2. Of those that a mesh axis runs over, the one named last changes fastest.
Arguments:
- sources: bfloat16 [4, 524288], P(None, ('grp', 'dev')), may hold values from -6 to 6
- self_near_block: bfloat16 [1024, 512, 512], P(('grp', 'dev')), may hold values from -0.1875 to 0.1875
- neighbour_near_block: bfloat16 [1024, 512, 512], P(('grp', 'dev')), may hold values from -0.1875 to 0.1875
- near_list: int32 [1024], P(('grp', 'dev')), may hold values from 0 to 1023, as said below
- bases: bfloat16 [1024, 64, 512], P(('grp', 'dev')), may hold values from -0.25 to 0.25
- far_leaf: int32 [1024, 16], P(('grp', 'dev')), may hold values from 0 to 1023, as said below
- far_count: int32 [1024], P(('grp', 'dev')), may hold values from 1 to 16, 8192 in all
- leaf_coupling: float32 [1024, 16, 64, 64], P(('grp', 'dev')), may hold values from -0.375 to 0.375
- leaf_transfer: float32 [1024, 64, 64], P(('grp', 'dev')), may hold values from -0.5 to 0.5
- far_cluster: int32 [256, 8], P(('grp', 'dev')), may hold values from 0 to 255, as said below
- cluster_coupling: float32 [256, 8, 64, 64], P(('grp', 'dev')), may hold values from -0.375 to 0.375
- cluster_transfer: float32 [256, 64, 64], P(('grp', 'dev')), may hold values from -0.375 to 0.375
- top_coupling: float32 [8, 8, 64, 64], P('grp'), may hold values from -0.375 to 0.375
Outputs:
- potential: float32 [4, 524288], P(None, ('grp', 'dev'))
The draws below stay inside these ranges and needn't reach their ends.
Inputs may be any that keep to these rules, and one draw needn't show every extreme that they name: near_list names a leaf held by the same device as the leaf or by one of the two devices beside it in the order of grp then dev. far_leaf names a leaf held by a device 2 to 3 places away from the leaf's own device in the order of grp then dev. far_cluster names a device cluster of the same group cluster as the row's own, never the row's own. Slots from far_count on are ignored.
All inputs are finite; a program needn't handle non-finite values. No bound on the sum of `far_count` on one device may be relied on, other than what follows from the above.
Results may differ from the reference program's by a relative error of at most 0.00045.
Values may be sent and summed in bfloat16 or wider, within the bound.
No kernel may reach another device: no remote copies, remote signals or barrier semaphores. Data moves between devices by JAX's collectives and lax.ppermute only.
A program may use at most 64 MiB of HBM per device.

```python
import math
import jax
import jax.numpy as jnp
import numpy as np
from jax import lax

LEAF = 512
RANK = 64
NVEC = 4
LPD = 4
FAR0 = 16
FAR1 = 8
FARW = 3
CLUSTERS = 256
LEAVES = 1024
PANELS = 524288
N_GRP = 8
N_DEV = 32


def draw_near_list(key, part):
    key = jax.random.fold_in(key, 11)
    initial_key, second_key = jax.random.split(key)
    devices_all = LEAVES // LPD
    holder = jnp.arange(LEAVES, dtype=jnp.int32) // LPD
    offset = jax.random.randint(initial_key, (LEAVES,), -1, 2, dtype=jnp.int32)
    target = jnp.clip(holder + offset, 0, devices_all - 1)
    within = jax.random.randint(second_key, (LEAVES,), 0, LPD, dtype=jnp.int32)
    chosen = (target * LPD + within).astype(jnp.int32)
    chosen = chosen.at[0].set(0)
    chosen = chosen.at[LEAVES - 1].set(LEAVES - 1)
    chosen = chosen.at[LPD].set(LPD - 1)
    chosen = chosen.at[LEAVES - 1 - LPD].set(LEAVES - LPD)
    return chosen.astype(jnp.int32)


def draw_far_leaf(key, part):
    key = jax.random.fold_in(key, 23)
    sign_key, reach_key, within_key = jax.random.split(key, 3)
    devices_all = LEAVES // LPD
    holder = (jnp.arange(LEAVES, dtype=jnp.int32) // LPD)[:, None]
    sign_pick = jax.random.randint(sign_key, (LEAVES, FAR0), 0, 2, dtype=jnp.int32) * 2 - 1
    reach = jax.random.randint(reach_key, (LEAVES, FAR0), 2, FARW + 1, dtype=jnp.int32)
    offset = sign_pick * reach
    target = holder + offset
    outside = jnp.logical_or(target < 0, target > devices_all - 1)
    target = jnp.where(outside, holder - offset, target)
    within = jax.random.randint(within_key, (LEAVES, FAR0), 0, LPD, dtype=jnp.int32)
    chosen = (target * LPD + within).astype(jnp.int32)
    chosen = chosen.at[0, 0].set(2 * LPD)
    chosen = chosen.at[LPD, 0].set((1 + FARW) * LPD)
    chosen = chosen.at[LEAVES - 1, 0].set((devices_all - 3) * LPD)
    chosen = chosen.at[(devices_all - 2) * LPD, 0].set((devices_all - 2 - FARW) * LPD)
    return chosen.astype(jnp.int32)


def draw_far_cluster(key, part):
    key = jax.random.fold_in(key, 37)
    own = jnp.arange(CLUSTERS, dtype=jnp.int32)[:, None]
    own_pos = own % N_DEV
    base = own - own_pos
    within = jax.random.randint(key, (CLUSTERS, FAR1), 0, N_DEV - 1, dtype=jnp.int32)
    within = within + (within >= own_pos).astype(jnp.int32)
    chosen = (base + within).astype(jnp.int32)
    chosen = chosen.at[1, 0].set(0)
    chosen = chosen.at[CLUSTERS - 2, 0].set(CLUSTERS - 1)
    return chosen.astype(jnp.int32)


def shard_levels(rng, extent, shards, least, largest):
    gain = 1.0
    for axis_at, blocks in shards:
        draws = jax.random.uniform(jax.random.fold_in(jax.random.fold_in(rng, 6), axis_at), (blocks,), jnp.float32, least / len(shards), largest / len(shards))
        gain = gain * jnp.repeat(jnp.exp(draws), extent[axis_at] // blocks).reshape((-1,) + (1,) * (len(extent) - 1 - axis_at))
    return gain


def split_up(count, total, bound, slope):
    weights = [(1 << 20) // math.isqrt(rank ** slope) + 1 for rank in range(2, count + 1)]
    surplus, given = total - bound - (count - 1), [1] * (count - 1)
    while surplus > 0:
        movable = [i for i in range(count - 1) if given[i] < bound]
        whole, remaining = sum([weights[i] for i in movable]), surplus
        for i in movable:
            addition = min(bound - given[i], max(1, remaining * weights[i] // whole), surplus)
            given[i] = given[i] + addition
            surplus = surplus - addition
    return np.array([bound] + given)


def uneven(key, count, total, bound, lean):
    if count == 2:
        one = jax.random.randint(key, (), max(1, total - bound), min(bound, total - 1) + 1)
        return jnp.stack([one, total - one])
    lengths = jnp.asarray(split_up(count, total, bound, lean), jnp.int32)
    pairs = (count - 1) // 2
    giver, receiver = lengths[1:1 + 2 * pairs:2], lengths[2:2 + 2 * pairs:2]
    margin = jnp.minimum(giver - 1, bound - receiver)
    moved = jax.random.randint(jax.random.fold_in(key, 1), (pairs,), 0, 1 << 20) % (margin + 1)
    lengths = lengths.at[1:1 + 2 * pairs:2].set(giver - moved).at[2:2 + 2 * pairs:2].set(receiver + moved)
    return lengths[jax.random.permutation(jax.random.fold_in(key, 2), count)]


def centred(key, shape, spread, most, cuts=(), kind=jnp.bfloat16):
    entries = jax.random.normal(key, shape, jnp.float32) * spread
    if len(cuts) > 0:
        entries = shard_levels(key, shape, cuts, -0.22, 0.18) * entries
    return jnp.clip(entries, min=-most, max=most).astype(kind)


def setup_inputs(seed: int = 0) -> dict:
    arg_keys = jax.random.split(jax.random.key(seed), 14)
    sources = centred(arg_keys[0], (NVEC, PANELS), 1.0, 6.0, ((1, 256),))
    self_near_block = centred(arg_keys[1], (LEAVES, LEAF, LEAF), (2 * LEAF) ** -0.5, 0.1875, ((0, 256),))
    neighbour_near_block = centred(arg_keys[2], (LEAVES, LEAF, LEAF), (2 * LEAF) ** -0.5, 0.1875, ((0, 256),))
    near_list = draw_near_list(jax.random.fold_in(arg_keys[13], 71), 0)
    bases = centred(arg_keys[4], (LEAVES, RANK, LEAF), LEAF ** -0.5, 0.25, ((0, 256),))
    far_leaf = draw_far_leaf(jax.random.fold_in(arg_keys[13], 71), 0)
    far_count = uneven(arg_keys[6], LEAVES, LEAVES * FAR0 // 2, FAR0, 2).astype(jnp.int32)
    leaf_coupling = centred(arg_keys[7], (LEAVES, FAR0, RANK, RANK), (4 * RANK) ** -0.5, 0.375, ((0, 256),), jnp.float32)
    leaf_transfer = centred(arg_keys[8], (LEAVES, RANK, RANK), (2 * RANK) ** -0.5, 0.5, ((0, 256),), jnp.float32)
    far_cluster = draw_far_cluster(jax.random.fold_in(arg_keys[13], 71), 0)
    cluster_coupling = centred(arg_keys[10], (CLUSTERS, FAR1, RANK, RANK), (4 * RANK) ** -0.5, 0.375, ((0, 256),), jnp.float32)
    cluster_transfer = centred(arg_keys[11], (CLUSTERS, RANK, RANK), (4 * RANK) ** -0.5, 0.375, ((0, 256),), jnp.float32)
    top_coupling = centred(arg_keys[12], (N_GRP, N_GRP, RANK, RANK), (4 * RANK) ** -0.5, 0.375, ((0, 8),), jnp.float32)
    return {"sources": sources, "self_near_block": self_near_block, "neighbour_near_block": neighbour_near_block, "near_list": near_list, "bases": bases, "far_leaf": far_leaf, "far_count": far_count, "leaf_coupling": leaf_coupling, "leaf_transfer": leaf_transfer, "far_cluster": far_cluster, "cluster_coupling": cluster_coupling, "cluster_transfer": cluster_transfer, "top_coupling": top_coupling}


HIGH = lax.Precision.HIGHEST


def reference(sources, self_near_block, neighbour_near_block, near_list, bases, far_leaf, far_count, leaf_coupling, leaf_transfer, far_cluster, cluster_coupling, cluster_transfer, top_coupling):
    leaves_all = LPD * N_GRP * N_DEV
    by_leaf = sources.reshape(NVEC, leaves_all, LEAF).transpose(1, 0, 2)
    adjacent_leaf = by_leaf[near_list]

    def near_one(pieces):
        self_block, other_block, own_rows, other_rows = pieces
        first = jnp.dot(own_rows, self_block.T, preferred_element_type=jnp.float32)
        second = jnp.dot(other_rows, other_block.T, preferred_element_type=jnp.float32)
        return first + second

    near_part = lax.map(near_one, (self_near_block, neighbour_near_block, by_leaf, adjacent_leaf))
    leaf_coeff = jnp.einsum('lvp,lkp->lvk', by_leaf.astype(jnp.float32), bases.astype(jnp.float32), precision=HIGH)
    leaf_terms = jnp.einsum('lkj,lvk->lvj', leaf_transfer, leaf_coeff, precision=HIGH)
    cluster_coeff = leaf_terms.reshape(N_GRP * N_DEV, LPD, NVEC, RANK).sum(axis=1)
    cluster_terms = jnp.einsum('dkj,dvk->dvj', cluster_transfer, cluster_coeff, precision=HIGH)
    group_coeff = cluster_terms.reshape(N_GRP, N_DEV, NVEC, RANK).sum(axis=1)
    off_mask = 1.0 - jnp.eye(N_GRP, dtype=jnp.float32)
    group_field = jnp.einsum('ghkj,hvj->gvk', top_coupling * off_mask[:, :, None, None], group_coeff, precision=HIGH)
    picked = cluster_coeff[far_cluster]
    cluster_far = jnp.einsum('dskj,dsvj->dvk', cluster_coupling, picked, precision=HIGH)
    group_of = jnp.repeat(group_field, N_DEV, axis=0)
    cluster_field = cluster_far + jnp.einsum('dkj,dvj->dvk', cluster_transfer, group_of, precision=HIGH)
    live_mask = (jnp.arange(FAR0, dtype=jnp.int32)[None, :] < far_count[:, None]).astype(jnp.float32)
    source_coeff = leaf_coeff[far_leaf] * live_mask[:, :, None, None]
    leaf_far = jnp.einsum('lskj,lsvj->lvk', leaf_coupling, source_coeff, precision=HIGH)
    cluster_of = jnp.repeat(cluster_field, LPD, axis=0)
    leaf_field = leaf_far + jnp.einsum('lkj,lvj->lvk', leaf_transfer, cluster_of, precision=HIGH)
    far_part = jnp.einsum('lkp,lvk->lvp', bases.astype(jnp.float32), leaf_field, precision=HIGH)
    total = near_part + far_part
    return total.transpose(1, 0, 2).reshape(NVEC, leaves_all * LEAF)
```

```python
import jax
import jax.numpy as jnp
from jax import lax
from jax.experimental import pallas as pl
from jax.experimental.pallas import tpu as pltpu
from jax.sharding import PartitionSpec as P

HIGH = lax.Precision.HIGHEST
F32 = jnp.float32
BF16 = jnp.bfloat16
LEAF = 512
RANK = 64
NVEC = 4
LPD = 4
FARW = 3
ROW = 2 * RANK + LPD * RANK
VMEM = pl.BlockSpec(memory_space=pltpu.VMEM)
SMEM = pl.BlockSpec(memory_space=pltpu.SMEM)


def rows_by_rows(a, b, precision=None):
    return lax.dot_general(
        a, b, (((1,), (1,)), ((), ())), precision=precision, preferred_element_type=F32
    )


def up_kernel(src, bases, leaf_transfer, cluster_transfer, out):
    leaf = [
        rows_by_rows(src[:, l * LEAF : (l + 1) * LEAF], bases[l]) for l in range(LPD)
    ]
    every = jnp.concatenate(leaf, axis=1)
    transfer = leaf_transfer[...].reshape(LPD * RANK, RANK)
    cluster = jnp.dot(every, transfer, precision=HIGH, preferred_element_type=F32)
    group = jnp.dot(cluster, cluster_transfer[0], precision=HIGH, preferred_element_type=F32)
    row = jnp.concatenate([cluster, group, every], axis=1)
    for i in range(out.shape[0]):
        out[i] = row


def group_kernel(first, out):
    d = lax.axis_index("dev")
    n_dev = first.shape[0]
    total = first[0, :, : 2 * RANK]
    for i in range(1, n_dev):
        total = total + first[i, :, : 2 * RANK]
    low = d <= FARW - 1
    a = jnp.where(low, jnp.minimum(n_dev - FARW + d, n_dev - 1), jnp.maximum(d - (n_dev - 2), 0))
    b = jnp.where(
        low, jnp.minimum(n_dev - FARW + 1 + d, n_dev - 1), jnp.maximum(d - (n_dev - FARW), 0)
    )
    row = jnp.concatenate([total, first[a, :, 2 * RANK :], first[b, :, 2 * RANK :]], axis=1)
    for i in range(out.shape[0]):
        out[i] = row


def lanes_to_matrix(sums):
    lane = lax.broadcasted_iota(jnp.int32, (RANK, 128), 1)
    out = jnp.zeros((RANK, 128), F32)
    for v, s in enumerate(sums):
        column = jnp.sum(s, axis=-1, keepdims=True).reshape(RANK, 1)
        out = jnp.where(lane == v, column, out)
    return out


def down_kernel(
    near_list,
    far_leaf,
    far_count,
    far_cluster,
    src,
    before,
    after,
    self_block,
    other_block,
    bases,
    leaf_coupling,
    leaf_transfer,
    cluster_coupling,
    cluster_transfer,
    top_coupling,
    first,
    second,
    out,
    table,
):
    g = lax.axis_index("grp")
    d = lax.axis_index("dev")
    n_dev = first.shape[0]
    n_grp = second.shape[0]
    me = g * n_dev + d

    near = []
    for l in range(LPD):
        here = near_list[l] - me * LPD + LPD
        at = pl.multiple_of((here % LPD) * LEAF, LEAF)
        which = here // LPD
        x0 = before[:, pl.ds(at, LEAF)]
        x1 = src[:, pl.ds(at, LEAF)]
        x2 = after[:, pl.ds(at, LEAF)]
        x = jnp.where(which == 0, x0, jnp.where(which == 1, x1, x2))
        near.append(
            rows_by_rows(src[:, l * LEAF : (l + 1) * LEAF], self_block[l])
            + rows_by_rows(x, other_block[l])
        )

    for pos, off in enumerate((-3, -2, 2, 3)):
        dd = d + off
        inside = jnp.logical_and(dd >= 0, dd < n_dev)
        own = first[dd & (n_dev - 1), :, 2 * RANK :]
        side = (g + (1 if off > 0 else -1)) & (n_grp - 1)
        start = 2 * RANK + (LPD * RANK if pos % 2 else 0)
        other = second[side, :, start : start + LPD * RANK]
        value = jnp.where(inside, own, other)
        for l in range(LPD):
            for v in range(NVEC):
                table[pos * LPD + l, v] = jnp.broadcast_to(
                    value[v : v + 1, l * RANK : (l + 1) * RANK], (8, RANK)
                )
    table[4 * LPD] = jnp.zeros((NVEC, 8, RANK), F32)

    def tiles(matrix):
        return matrix.reshape(RANK // 8, 8, RANK)

    sums = [jnp.zeros((RANK // 8, 8, RANK), F32) for _ in range(NVEC)]
    for h in range(n_grp):
        c = tiles(top_coupling[0, h])
        x = jnp.where(h != g, second[h, :, RANK : 2 * RANK], 0.0)
        for v in range(NVEC):
            sums[v] = sums[v] + c * jnp.broadcast_to(x[v : v + 1], (8, RANK))[None]
    group_field = lanes_to_matrix(sums)

    sums = [jnp.zeros((RANK // 8, 8, RANK), F32) for _ in range(NVEC)]
    for s in range(far_cluster.shape[1]):
        c = tiles(cluster_coupling[0, s])
        x = first[far_cluster[0, s] & (n_dev - 1), :, :RANK]
        for v in range(NVEC):
            sums[v] = sums[v] + c * jnp.broadcast_to(x[v : v + 1], (8, RANK))[None]
    cluster_field = lanes_to_matrix(sums) + jnp.dot(
        cluster_transfer[0], group_field, precision=HIGH, preferred_element_type=F32
    )
    from_cluster = jnp.dot(
        leaf_transfer[...].reshape(LPD * RANK, RANK),
        cluster_field,
        precision=HIGH,
        preferred_element_type=F32,
    )

    for l in range(LPD):
        sums = [jnp.zeros((RANK // 8, 8, RANK), F32) for _ in range(NVEC)]
        for s in range(far_leaf.shape[1]):
            leaf = far_leaf[l, s]
            delta = (leaf >> 2) - me
            pos = jnp.where(delta < 0, delta + FARW, delta)
            at = jnp.where(s < far_count[l], pos * LPD + (leaf & (LPD - 1)), 4 * LPD)
            c = tiles(leaf_coupling[l, s])
            for v in range(NVEC):
                sums[v] = sums[v] + c * table[at, v][None]
        field = lanes_to_matrix(sums) + from_cluster[l * RANK : (l + 1) * RANK]
        field = jnp.transpose(field)[:8]
        high = field.astype(BF16).astype(F32)
        middle = (field - high).astype(BF16).astype(F32)
        low = field - high - middle
        parts = jnp.concatenate([high, middle, low, jnp.zeros_like(low)], axis=0).astype(BF16)
        far = jnp.dot(parts, bases[l], preferred_element_type=F32)
        far = far[:8] + far[8:16] + far[16:24]
        out[:, l * LEAF : (l + 1) * LEAF] = near[l] + far[:NVEC]


def shift(value, axis, steps):
    count = lax.axis_size(axis)
    return lax.ppermute(value, axis, [(i, (i + steps) % count) for i in range(count)])


def per_device(
    sources,
    self_near_block,
    neighbour_near_block,
    near_list,
    bases,
    far_leaf,
    far_count,
    leaf_coupling,
    leaf_transfer,
    far_cluster,
    cluster_coupling,
    cluster_transfer,
    top_coupling,
):
    n_dev = lax.axis_size("dev")
    n_grp = lax.axis_size("grp")
    before = shift(sources, ("grp", "dev"), 1)
    after = shift(sources, ("grp", "dev"), -1)
    row = pl.pallas_call(
        up_kernel,
        out_shape=jax.ShapeDtypeStruct((n_dev, NVEC, ROW), F32),
        in_specs=[VMEM] * 4,
        out_specs=VMEM,
        name="up",
    )(sources, bases, leaf_transfer, cluster_transfer)
    first = lax.all_to_all(row, "dev", 0, 0)
    row = pl.pallas_call(
        group_kernel,
        out_shape=jax.ShapeDtypeStruct((n_grp, NVEC, 2 * RANK + 2 * LPD * RANK), F32),
        in_specs=[VMEM],
        out_specs=VMEM,
        name="group",
    )(first)
    second = lax.all_to_all(row, "grp", 0, 0)
    return pl.pallas_call(
        down_kernel,
        out_shape=jax.ShapeDtypeStruct(sources.shape, F32),
        in_specs=[SMEM] * 4 + [VMEM] * 13,
        out_specs=VMEM,
        scratch_shapes=[pltpu.VMEM((4 * LPD + 1, NVEC, 8, RANK), F32)],
        compiler_params=pltpu.CompilerParams(vmem_limit_bytes=24 * 1024 * 1024),
        name="down",
    )(
        near_list,
        far_leaf,
        far_count,
        far_cluster,
        sources,
        before,
        after,
        self_near_block,
        neighbour_near_block,
        bases,
        leaf_coupling,
        leaf_transfer,
        cluster_coupling,
        cluster_transfer,
        top_coupling,
        first,
        second,
    )


def solution(mesh):
    placed = (
        P(None, ("grp", "dev")),
        P(("grp", "dev"), None, None),
        P(("grp", "dev"), None, None),
        P(("grp", "dev")),
        P(("grp", "dev"), None, None),
        P(("grp", "dev"), None),
        P(("grp", "dev")),
        P(("grp", "dev"), None, None, None),
        P(("grp", "dev"), None, None),
        P(("grp", "dev"), None),
        P(("grp", "dev"), None, None, None),
        P(("grp", "dev"), None, None),
        P("grp", None, None, None),
    )
    return jax.shard_map(
        per_device, mesh=mesh, in_specs=placed, out_specs=P(None, ("grp", "dev")), check_vma=False
    )
```

```python
import jax
import jax.numpy as jnp
from jax import lax
from jax.experimental import pallas as pl
from jax.experimental.pallas import tpu as pltpu
from jax.sharding import PartitionSpec as P

HIGH = lax.Precision.HIGHEST
F32 = jnp.float32
BF16 = jnp.bfloat16
LEAF = 512
RANK = 64
NVEC = 4
LPD = 4
FARW = 3
WIDE = LPD * RANK
VMEM = pl.BlockSpec(memory_space=pltpu.VMEM)
HBM = pl.BlockSpec(memory_space=pltpu.HBM)
SMEM = pl.BlockSpec(memory_space=pltpu.SMEM)


def rows_by_rows(a, b, precision=None):
    return lax.dot_general(
        a, b, (((1,), (1,)), ((), ())), precision=precision, preferred_element_type=F32
    )


def exact_dot(a, b):
    return jnp.dot(a, b, precision=HIGH, preferred_element_type=F32)


def parts_of(rows):
    high = rows.astype(BF16).astype(F32)
    middle = (rows - high).astype(BF16).astype(F32)
    low = rows - high - middle
    return jnp.concatenate([high, middle, low, jnp.zeros_like(low)], axis=0).astype(BF16)


def tiles(matrix):
    return matrix.reshape(RANK // 8, 8, RANK)


def no_sums():
    return [jnp.zeros((RANK // 8, 8, RANK), F32) for _ in range(NVEC)]


def lanes_to_matrix(sums):
    lane = lax.broadcasted_iota(jnp.int32, (RANK, 128), 1)
    out = jnp.zeros((RANK, 128), F32)
    for v, s in enumerate(sums):
        column = jnp.sum(s, axis=-1, keepdims=True).reshape(RANK, 1)
        out = jnp.where(lane == v, column, out)
    return out


def spread(rows, v):
    return jnp.broadcast_to(rows[v : v + 1], (8, RANK))


def up_kernel(
    src_h, bases_h, leaf_h, cluster_h, self_h, send, self_block, src, bases, leaf, cluster, sem
):
    copies = [
        pltpu.make_async_copy(a, b, sem.at[i])
        for i, (a, b) in enumerate(
            (
                (leaf_h, leaf),
                (cluster_h, cluster),
                (src_h, src),
                (bases_h, bases),
                (self_h, self_block),
            )
        )
    ]
    for c in copies:
        c.start()
    copies[0].wait()
    copies[1].wait()
    to_cluster = leaf[...].reshape(WIDE, RANK)
    to_group = exact_dot(to_cluster, cluster[0])
    both = jnp.concatenate([to_cluster, to_group], axis=1)
    copies[2].wait()
    copies[3].wait()
    every = jnp.concatenate(
        [rows_by_rows(src[:, l * LEAF : (l + 1) * LEAF], bases[l]) for l in range(LPD)], axis=1
    )
    row = jnp.concatenate([exact_dot(every, both), every], axis=1)
    for i in range(send.shape[0]):
        send[i] = row
    copies[4].wait()


def near_kernel(near_list, src, odd_swap, even_swap, self_block, other_h, near, block, sem):
    copies = [
        pltpu.make_async_copy(other_h.at[l], block.at[l], sem.at[l]) for l in range(LPD)
    ]
    for c in copies:
        c.start()
    me = lax.axis_index("grp") * lax.axis_size("dev") + lax.axis_index("dev")
    is_odd = (me & 1) == 1
    own = [
        rows_by_rows(src[:, l * LEAF : (l + 1) * LEAF], self_block[l]) for l in range(LPD)
    ]
    for l in range(LPD):
        here = jnp.clip(near_list[l] - me * LPD + LPD, 0, 3 * LPD - 1)
        at = pl.multiple_of((here & (LPD - 1)) * LEAF, LEAF)
        which = here >> 2
        x1 = src[:, pl.ds(at, LEAF)]
        x2 = odd_swap[:, pl.ds(at, LEAF)]
        x3 = even_swap[:, pl.ds(at, LEAF)]
        x = jnp.where(which == 1, x1, jnp.where((which == 0) == is_odd, x2, x3))
        copies[l].wait()
        near[:, l * LEAF : (l + 1) * LEAF] = own[l] + rows_by_rows(x, block[l])


def group_kernel(first, send):
    d = lax.axis_index("dev")
    n_dev = first.shape[0]
    total = jnp.sum(first[:, :, : 2 * RANK], axis=0)
    low = d < FARW
    a = jnp.where(low, jnp.minimum(n_dev - FARW + d, n_dev - 1), jnp.maximum(d - (n_dev - 2), 0))
    b = jnp.where(
        low, jnp.minimum(n_dev - FARW + 1 + d, n_dev - 1), jnp.maximum(d - (n_dev - FARW), 0)
    )
    row = jnp.concatenate([total, first[a, :, 2 * RANK :], first[b, :, 2 * RANK :]], axis=1)
    for i in range(send.shape[0]):
        send[i] = row


def far_sums(coupling, l, table, entry):
    sums = no_sums()
    for s in range(coupling.shape[1]):
        c = tiles(coupling[l, s])
        at = entry(l, s)
        for v in range(NVEC):
            sums[v] = sums[v] + c * table[at, v][None]
    return lanes_to_matrix(sums)


def fill(table, first_entry, value):
    for l in range(LPD):
        for v in range(NVEC):
            table[first_entry + l, v] = spread(value[:, l * RANK : (l + 1) * RANK], v)


def mid_kernel(
    far_leaf, far_count, far_cluster, first, near, leaf_h, transfer_h, bases_h, coupling_h,
    cluster_h, top_h, base, down_high, down_low, bases, coupling, top_out, leaf_transfer, transfer,
    cluster, table, sem
):
    copies = []
    for a, b in (
        [(leaf_h, leaf_transfer), (transfer_h, transfer), (cluster_h, cluster)]
        + [(bases_h, bases)]
        + [(coupling_h.at[l], coupling.at[l]) for l in range(LPD)]
        + [(top_h, top_out)]
    ):
        copy = pltpu.make_async_copy(a, b, sem.at[len(copies)])
        copy.start()
        copies.append(copy)
    d = lax.axis_index("dev")
    n_dev = lax.axis_size("dev")
    me = lax.axis_index("grp") * n_dev + d

    for pos, off in enumerate((-3, -2, 2, 3)):
        fill(table, pos * LPD, first[jnp.clip(d + off, 0, n_dev - 1), :, 2 * RANK :])
    table[4 * LPD] = jnp.zeros((NVEC, 8, RANK), F32)

    for c in copies[:3]:
        c.wait()
    to_cluster = leaf_transfer[...].reshape(WIDE, RANK)
    to_group = exact_dot(to_cluster, transfer[0])
    high = to_group.astype(BF16)
    down_high[...] = high
    down_low[...] = (to_group - high.astype(F32)).astype(BF16)
    sums = no_sums()
    for s in range(far_cluster.shape[1]):
        c = tiles(cluster[0, s])
        x = first[far_cluster[0, s] & (n_dev - 1), :, :RANK]
        for v in range(NVEC):
            sums[v] = sums[v] + c * spread(x, v)[None]
    from_cluster = exact_dot(to_cluster, lanes_to_matrix(sums))

    def entry(l, s):
        leaf = far_leaf[l, s]
        delta = (leaf >> 2) - me
        pos = jnp.where(delta < 0, delta + FARW, delta)
        here = jnp.logical_and(d + delta >= 0, d + delta < n_dev)
        live = jnp.logical_and(s < far_count[l], here)
        return jnp.clip(jnp.where(live, pos * LPD + (leaf & (LPD - 1)), 4 * LPD), 0, 4 * LPD)

    copies[3].wait()
    for l in range(LPD):
        copies[4 + l].wait()
        field = far_sums(coupling, l, table, entry) + from_cluster[l * RANK : (l + 1) * RANK]
        product = jnp.dot(
            parts_of(jnp.transpose(field)[:8]), bases[l], preferred_element_type=F32
        )
        product = product[:8] + product[8:16] + product[16:24]
        at = slice(l * LEAF, (l + 1) * LEAF)
        base[:, at] = near[:, at] + product[:NVEC]
    copies[4 + LPD].wait()


def down_kernel(
    far_leaf, far_count, base, down_high, down_low, bases, coupling, top_coupling, second, out,
    table, extra
):
    g = lax.axis_index("grp")
    d = lax.axis_index("dev")
    n_dev = lax.axis_size("dev")
    n_grp = second.shape[0]
    me = g * n_dev + d
    extra[...] = jnp.zeros(extra.shape, F32)

    @pl.when(jnp.logical_or(d < FARW, d >= n_dev - FARW))
    def _():
        side = (g + jnp.where(d < FARW, -1, 1)) & (n_grp - 1)
        for k in range(2):
            start = 2 * RANK + k * WIDE
            fill(table, k * LPD, second[side, :, start : start + WIDE])
        table[2 * LPD] = jnp.zeros((NVEC, 8, RANK), F32)

        def entry(l, s):
            leaf = far_leaf[l, s]
            delta = (leaf >> 2) - me
            which = jnp.where(delta < 0, delta + FARW, delta) & 1
            there = jnp.logical_or(d + delta < 0, d + delta >= n_dev)
            live = jnp.logical_and(s < far_count[l], there)
            return jnp.where(live, which * LPD + (leaf & (LPD - 1)), 2 * LPD)

        for l in range(LPD):
            field = jnp.transpose(far_sums(coupling, l, table, entry))[:8]
            extra[:, l * RANK : (l + 1) * RANK] = field

    sums = no_sums()
    for h in range(n_grp):
        c = tiles(top_coupling[0, h])
        x = jnp.where(h != g, second[h, :, RANK : 2 * RANK], 0.0)
        for v in range(NVEC):
            sums[v] = sums[v] + c * spread(x, v)[None]
    parts = parts_of(jnp.transpose(lanes_to_matrix(sums))[:8])
    field = rows_by_rows(parts, down_high[...])
    field = field[:8] + field[8:16] + field[16:24] + rows_by_rows(parts[:16], down_low[...])[:8]
    parts = parts_of(field + extra[...])
    for l in range(LPD):
        far = jnp.dot(parts[:, l * RANK : (l + 1) * RANK], bases[l], preferred_element_type=F32)
        far = far[:8] + far[8:16] + far[16:24]
        at = slice(l * LEAF, (l + 1) * LEAF)
        out[:, at] = base[:, at] + far[:NVEC]


def permute(value, pairs):
    return lax.ppermute(value, ("grp", "dev"), pairs)


def swapped(value, start, count):
    pairs = [(i, (i + 1) % count) for i in range(start, count, 2)]
    return lax.ppermute(value, ("grp", "dev"), pairs + [(j, i) for i, j in pairs])


def in_hbm(*arrays):
    return [pltpu.with_memory_space_constraint(a, pltpu.HBM) for a in arrays]


def params(mib):
    return pltpu.CompilerParams(vmem_limit_bytes=mib * 1024 * 1024)


def cost(flops, size):
    return pl.CostEstimate(flops=flops, bytes_accessed=size, transcendentals=0)


def per_device(
    sources,
    self_near_block,
    neighbour_near_block,
    near_list,
    bases,
    far_leaf,
    far_count,
    leaf_coupling,
    leaf_transfer,
    far_cluster,
    cluster_coupling,
    cluster_transfer,
    top_coupling,
):
    n_dev = lax.axis_size("dev")
    n_grp = lax.axis_size("grp")
    n_all = n_dev * n_grp
    sds = jax.ShapeDtypeStruct
    send, self_v = pl.pallas_call(
        up_kernel,
        out_shape=[
            sds((n_dev, NVEC, 2 * RANK + WIDE), F32),
            sds(self_near_block.shape, BF16),
        ],
        in_specs=[HBM] * 5,
        out_specs=[VMEM] * 2,
        scratch_shapes=[
            pltpu.VMEM(sources.shape, BF16),
            pltpu.VMEM(bases.shape, BF16),
            pltpu.VMEM(leaf_transfer.shape, F32),
            pltpu.VMEM(cluster_transfer.shape, F32),
            pltpu.SemaphoreType.DMA((5,)),
        ],
        compiler_params=params(8),
        name="up",
    )(*in_hbm(sources, bases, leaf_transfer, cluster_transfer, self_near_block))
    first = lax.all_to_all(send, "dev", 0, 0)
    send, tied = lax.optimization_barrier((send, sources))
    odd_swap, even_swap = swapped(tied, 0, n_all), swapped(tied, 1, n_all)
    near = pl.pallas_call(
        near_kernel,
        out_shape=sds(sources.shape, F32),
        in_specs=[SMEM] + [VMEM] * 4 + [HBM],
        out_specs=VMEM,
        scratch_shapes=[
            pltpu.VMEM(neighbour_near_block.shape, BF16),
            pltpu.SemaphoreType.DMA((LPD,)),
        ],
        compiler_params=params(8),
        cost_estimate=cost(40000000, 4000000),
        name="near",
    )(
        *in_hbm(near_list, sources),
        odd_swap,
        even_swap,
        self_v,
        *in_hbm(neighbour_near_block),
    )
    first, near = lax.optimization_barrier((first, near))
    send = pl.pallas_call(
        group_kernel,
        out_shape=sds((n_grp, NVEC, 2 * RANK + 2 * WIDE), F32),
        in_specs=[VMEM],
        out_specs=VMEM,
        compiler_params=params(4),
        name="group",
    )(first)
    second = lax.all_to_all(send, "grp", 0, 0)
    base, down_high, down_low, bases_v, coupling_v, top_v = pl.pallas_call(
        mid_kernel,
        out_shape=[
            sds(sources.shape, F32),
            sds((WIDE, RANK), BF16),
            sds((WIDE, RANK), BF16),
            sds(bases.shape, BF16),
            sds(leaf_coupling.shape, F32),
            sds(top_coupling.shape, F32),
        ],
        in_specs=[SMEM] * 3 + [VMEM] * 2 + [HBM] * 6,
        out_specs=[VMEM] * 6,
        scratch_shapes=[
            pltpu.VMEM(leaf_transfer.shape, F32),
            pltpu.VMEM(cluster_transfer.shape, F32),
            pltpu.VMEM(cluster_coupling.shape, F32),
            pltpu.VMEM((4 * LPD + 1, NVEC, 8, RANK), F32),
            pltpu.SemaphoreType.DMA((5 + LPD,)),
        ],
        compiler_params=params(12),
        cost_estimate=cost(40000000, 5000000),
        name="mid",
    )(
        *in_hbm(far_leaf, far_count, far_cluster),
        first,
        near,
        *in_hbm(
            leaf_transfer, cluster_transfer, bases, leaf_coupling, cluster_coupling, top_coupling
        ),
    )
    return pl.pallas_call(
        down_kernel,
        out_shape=sds(sources.shape, F32),
        in_specs=[SMEM] * 2 + [VMEM] * 7,
        out_specs=VMEM,
        scratch_shapes=[
            pltpu.VMEM((2 * LPD + 1, NVEC, 8, RANK), F32),
            pltpu.VMEM((8, WIDE), F32),
        ],
        compiler_params=params(8),
        name="down",
    )(
        *in_hbm(far_leaf, far_count),
        base,
        down_high,
        down_low,
        bases_v,
        coupling_v,
        top_v,
        second,
    )


def solution(mesh):
    placed = (
        P(None, ("grp", "dev")),
        P(("grp", "dev"), None, None),
        P(("grp", "dev"), None, None),
        P(("grp", "dev")),
        P(("grp", "dev"), None, None),
        P(("grp", "dev"), None),
        P(("grp", "dev")),
        P(("grp", "dev"), None, None, None),
        P(("grp", "dev"), None, None),
        P(("grp", "dev"), None),
        P(("grp", "dev"), None, None, None),
        P(("grp", "dev"), None, None),
        P("grp", None, None, None),
    )
    return jax.shard_map(
        per_device, mesh=mesh, in_specs=placed, out_specs=P(None, ("grp", "dev")), check_vma=False
    )
```

```python
import jax
import jax.numpy as jnp
from jax import lax
from jax.experimental import pallas as pl
from jax.experimental.pallas import tpu as pltpu
from jax.sharding import PartitionSpec as P

HIGH = lax.Precision.HIGHEST
F32 = jnp.float32
BF16 = jnp.bfloat16
LEAF = 512
RANK = 64
NVEC = 4
LPD = 4
FARW = 3
WIDE = LPD * RANK
VMEM = pl.BlockSpec(memory_space=pltpu.VMEM)
HBM = pl.BlockSpec(memory_space=pltpu.HBM)
SMEM = pl.BlockSpec(memory_space=pltpu.SMEM)


def rows_by_rows(a, b, precision=None):
    return lax.dot_general(
        a, b, (((1,), (1,)), ((), ())), precision=precision, preferred_element_type=F32
    )


def exact_dot(a, b):
    return jnp.dot(a, b, precision=HIGH, preferred_element_type=F32)


def parts_of(rows):
    high = rows.astype(BF16).astype(F32)
    middle = (rows - high).astype(BF16).astype(F32)
    low = rows - high - middle
    return jnp.concatenate([high, middle, low, jnp.zeros_like(low)], axis=0).astype(BF16)


def tiles(matrix):
    return matrix.reshape(RANK // 8, 8, RANK)


def no_sums():
    return [jnp.zeros((RANK // 8, 8, RANK), F32) for _ in range(NVEC)]


def lanes_to_matrix(sums):
    lane = lax.broadcasted_iota(jnp.int32, (RANK, 128), 1)
    out = jnp.zeros((RANK, 128), F32)
    for v, s in enumerate(sums):
        column = jnp.sum(s, axis=-1, keepdims=True).reshape(RANK, 1)
        out = jnp.where(lane == v, column, out)
    return out


def spread(rows, v):
    return jnp.broadcast_to(rows[v : v + 1], (8, RANK))


def up_kernel(
    src_h, bases_h, leaf_h, cluster_h, send, src, bases, leaf, cluster, sem
):
    copies = [
        pltpu.make_async_copy(a, b, sem.at[i])
        for i, (a, b) in enumerate(
            (
                (leaf_h, leaf),
                (cluster_h, cluster),
                (src_h, src),
                (bases_h, bases),
            )
        )
    ]
    for c in copies:
        c.start()
    copies[0].wait()
    copies[1].wait()
    to_cluster = leaf[...].reshape(WIDE, RANK)
    to_group = exact_dot(to_cluster, cluster[0])
    both = jnp.concatenate([to_cluster, to_group], axis=1)
    copies[2].wait()
    copies[3].wait()
    every = jnp.concatenate(
        [rows_by_rows(src[:, l * LEAF : (l + 1) * LEAF], bases[l]) for l in range(LPD)], axis=1
    )
    row = jnp.concatenate([exact_dot(every, both), every], axis=1)
    for i in range(send.shape[0]):
        send[i] = row


def own_kernel(src, self_h, other_h, own, other, block, sem):
    copies = [
        pltpu.make_async_copy(self_h.at[l], block.at[l], sem.at[l]) for l in range(LPD)
    ] + [pltpu.make_async_copy(other_h, other, sem.at[LPD])]
    for c in copies:
        c.start()
    for l in range(LPD):
        at = slice(l * LEAF, (l + 1) * LEAF)
        copies[l].wait()
        own[:, at] = rows_by_rows(src[:, at], block[l])
    copies[LPD].wait()


def near_kernel(near_list, src, even_swap, odd_swap, own, other, near):
    me = lax.axis_index("grp") * lax.axis_size("dev") + lax.axis_index("dev")
    is_odd = (me & 1) == 1
    for l in range(LPD):
        here = jnp.clip(near_list[l] - me * LPD + LPD, 0, 3 * LPD - 1)
        at = pl.multiple_of((here & (LPD - 1)) * LEAF, LEAF)
        which = here >> 2
        x1 = src[:, pl.ds(at, LEAF)]
        x2 = odd_swap[:, pl.ds(at, LEAF)]
        x3 = even_swap[:, pl.ds(at, LEAF)]
        x = jnp.where(which == 1, x1, jnp.where((which == 0) == is_odd, x2, x3))
        at = slice(l * LEAF, (l + 1) * LEAF)
        near[:, at] = own[:, at] + rows_by_rows(x, other[l])


def group_kernel(first, send):
    d = lax.axis_index("dev")
    n_dev = first.shape[0]
    total = jnp.sum(first[:, :, : 2 * RANK], axis=0)
    low = d < FARW
    a = jnp.where(low, jnp.minimum(n_dev - FARW + d, n_dev - 1), jnp.maximum(d - (n_dev - 2), 0))
    b = jnp.where(
        low, jnp.minimum(n_dev - FARW + 1 + d, n_dev - 1), jnp.maximum(d - (n_dev - FARW), 0)
    )
    row = jnp.concatenate([total, first[a, :, 2 * RANK :], first[b, :, 2 * RANK :]], axis=1)
    for i in range(send.shape[0]):
        send[i] = row


def far_sums(coupling, l, table, entry):
    sums = no_sums()
    for s in range(coupling.shape[1]):
        c = tiles(coupling[l, s])
        at = entry(l, s)
        for v in range(NVEC):
            sums[v] = sums[v] + c * table[at, v][None]
    return lanes_to_matrix(sums)


def fill(table, first_entry, value):
    for l in range(LPD):
        for v in range(NVEC):
            table[first_entry + l, v] = spread(value[:, l * RANK : (l + 1) * RANK], v)


def mid_kernel(
    far_leaf, far_count, far_cluster, first, near, leaf_h, transfer_h, bases_h, coupling_h,
    cluster_h, top_h, base, down_high, down_low, bases, coupling, top_out, leaf_transfer, transfer,
    cluster, table, sem
):
    copies = []
    for a, b in (
        [(leaf_h, leaf_transfer), (transfer_h, transfer), (cluster_h, cluster)]
        + [(bases_h, bases)]
        + [(coupling_h.at[l], coupling.at[l]) for l in range(LPD)]
        + [(top_h, top_out)]
    ):
        copy = pltpu.make_async_copy(a, b, sem.at[len(copies)])
        copy.start()
        copies.append(copy)
    d = lax.axis_index("dev")
    n_dev = lax.axis_size("dev")
    me = lax.axis_index("grp") * n_dev + d

    for pos, off in enumerate((-3, -2, 2, 3)):
        fill(table, pos * LPD, first[jnp.clip(d + off, 0, n_dev - 1), :, 2 * RANK :])
    table[4 * LPD] = jnp.zeros((NVEC, 8, RANK), F32)

    for c in copies[:3]:
        c.wait()
    to_cluster = leaf_transfer[...].reshape(WIDE, RANK)
    to_group = exact_dot(to_cluster, transfer[0])
    high = to_group.astype(BF16)
    down_high[...] = high
    down_low[...] = (to_group - high.astype(F32)).astype(BF16)
    sums = no_sums()
    for s in range(far_cluster.shape[1]):
        c = tiles(cluster[0, s])
        x = first[far_cluster[0, s] & (n_dev - 1), :, :RANK]
        for v in range(NVEC):
            sums[v] = sums[v] + c * spread(x, v)[None]
    from_cluster = exact_dot(to_cluster, lanes_to_matrix(sums))

    def entry(l, s):
        leaf = far_leaf[l, s]
        delta = (leaf >> 2) - me
        pos = jnp.where(delta < 0, delta + FARW, delta)
        here = jnp.logical_and(d + delta >= 0, d + delta < n_dev)
        live = jnp.logical_and(s < far_count[l], here)
        return jnp.clip(jnp.where(live, pos * LPD + (leaf & (LPD - 1)), 4 * LPD), 0, 4 * LPD)

    copies[3].wait()
    for l in range(LPD):
        copies[4 + l].wait()
        field = far_sums(coupling, l, table, entry) + from_cluster[l * RANK : (l + 1) * RANK]
        product = jnp.dot(
            parts_of(jnp.transpose(field)[:8]), bases[l], preferred_element_type=F32
        )
        product = product[:8] + product[8:16] + product[16:24]
        at = slice(l * LEAF, (l + 1) * LEAF)
        base[:, at] = near[:, at] + product[:NVEC]
    copies[4 + LPD].wait()


def down_kernel(
    far_leaf, far_count, base, down_high, down_low, bases, coupling, top_coupling, second, out,
    table, extra
):
    g = lax.axis_index("grp")
    d = lax.axis_index("dev")
    n_dev = lax.axis_size("dev")
    n_grp = second.shape[0]
    me = g * n_dev + d
    extra[...] = jnp.zeros(extra.shape, F32)

    @pl.when(jnp.logical_or(d < FARW, d >= n_dev - FARW))
    def _():
        side = (g + jnp.where(d < FARW, -1, 1)) & (n_grp - 1)
        for k in range(2):
            start = 2 * RANK + k * WIDE
            fill(table, k * LPD, second[side, :, start : start + WIDE])
        table[2 * LPD] = jnp.zeros((NVEC, 8, RANK), F32)

        def entry(l, s):
            leaf = far_leaf[l, s]
            delta = (leaf >> 2) - me
            which = jnp.where(delta < 0, delta + FARW, delta) & 1
            there = jnp.logical_or(d + delta < 0, d + delta >= n_dev)
            live = jnp.logical_and(s < far_count[l], there)
            return jnp.where(live, which * LPD + (leaf & (LPD - 1)), 2 * LPD)

        for l in range(LPD):
            field = jnp.transpose(far_sums(coupling, l, table, entry))[:8]
            extra[:, l * RANK : (l + 1) * RANK] = field

    sums = no_sums()
    for h in range(n_grp):
        c = tiles(top_coupling[0, h])
        x = jnp.where(h != g, second[h, :, RANK : 2 * RANK], 0.0)
        for v in range(NVEC):
            sums[v] = sums[v] + c * spread(x, v)[None]
    parts = parts_of(jnp.transpose(lanes_to_matrix(sums))[:8])
    field = rows_by_rows(parts, down_high[...])
    field = field[:8] + field[8:16] + field[16:24] + rows_by_rows(parts[:16], down_low[...])[:8]
    parts = parts_of(field + extra[...])
    for l in range(LPD):
        far = jnp.dot(parts[:, l * RANK : (l + 1) * RANK], bases[l], preferred_element_type=F32)
        far = far[:8] + far[8:16] + far[16:24]
        at = slice(l * LEAF, (l + 1) * LEAF)
        out[:, at] = base[:, at] + far[:NVEC]


def permute(value, pairs):
    return lax.ppermute(value, ("grp", "dev"), pairs)


def swapped(value, start, count):
    pairs = [(i, (i + 1) % count) for i in range(start, count, 2)]
    return lax.ppermute(value, ("grp", "dev"), pairs + [(j, i) for i, j in pairs])


def in_hbm(*arrays):
    return [pltpu.with_memory_space_constraint(a, pltpu.HBM) for a in arrays]


def params(mib):
    return pltpu.CompilerParams(vmem_limit_bytes=mib * 1024 * 1024)


def cost(flops, size):
    return pl.CostEstimate(flops=flops, bytes_accessed=size, transcendentals=0)


def per_device(
    sources,
    self_near_block,
    neighbour_near_block,
    near_list,
    bases,
    far_leaf,
    far_count,
    leaf_coupling,
    leaf_transfer,
    far_cluster,
    cluster_coupling,
    cluster_transfer,
    top_coupling,
):
    n_dev = lax.axis_size("dev")
    n_grp = lax.axis_size("grp")
    n_all = n_dev * n_grp
    sds = jax.ShapeDtypeStruct
    send = pl.pallas_call(
        up_kernel,
        out_shape=sds((n_dev, NVEC, 2 * RANK + WIDE), F32),
        in_specs=[HBM] * 4,
        out_specs=VMEM,
        scratch_shapes=[
            pltpu.VMEM(sources.shape, BF16),
            pltpu.VMEM(bases.shape, BF16),
            pltpu.VMEM(leaf_transfer.shape, F32),
            pltpu.VMEM(cluster_transfer.shape, F32),
            pltpu.SemaphoreType.DMA((4,)),
        ],
        compiler_params=params(8),
        name="up",
    )(*in_hbm(sources, bases, leaf_transfer, cluster_transfer))
    first = lax.all_to_all(send, "dev", 0, 0)
    send, tied = lax.optimization_barrier((send, sources))
    even_swap = swapped(tied, 1, n_all)
    odd_swap = swapped(tied, 0, n_all)
    own, other_v = pl.pallas_call(
        own_kernel,
        out_shape=[sds(sources.shape, F32), sds(neighbour_near_block.shape, BF16)],
        in_specs=[VMEM] + [HBM] * 2,
        out_specs=[VMEM] * 2,
        scratch_shapes=[
            pltpu.VMEM(self_near_block.shape, BF16),
            pltpu.SemaphoreType.DMA((1 + LPD,)),
        ],
        compiler_params=params(8),
        cost_estimate=cost(20000000, 4000000),
        name="own",
    )(*in_hbm(tied, self_near_block, neighbour_near_block))
    near = pl.pallas_call(
        near_kernel,
        out_shape=sds(sources.shape, F32),
        in_specs=[SMEM] + [VMEM] * 5,
        out_specs=VMEM,
        compiler_params=params(4),
        cost_estimate=cost(20000000, 2000000),
        name="near",
    )(*in_hbm(near_list, tied), even_swap, odd_swap, own, other_v)
    first, near = lax.optimization_barrier((first, near))
    send = pl.pallas_call(
        group_kernel,
        out_shape=sds((n_grp, NVEC, 2 * RANK + 2 * WIDE), F32),
        in_specs=[VMEM],
        out_specs=VMEM,
        compiler_params=params(4),
        name="group",
    )(first)
    second = lax.all_to_all(send, "grp", 0, 0)
    base, down_high, down_low, bases_v, coupling_v, top_v = pl.pallas_call(
        mid_kernel,
        out_shape=[
            sds(sources.shape, F32),
            sds((WIDE, RANK), BF16),
            sds((WIDE, RANK), BF16),
            sds(bases.shape, BF16),
            sds(leaf_coupling.shape, F32),
            sds(top_coupling.shape, F32),
        ],
        in_specs=[SMEM] * 3 + [VMEM] * 2 + [HBM] * 6,
        out_specs=[VMEM] * 6,
        scratch_shapes=[
            pltpu.VMEM(leaf_transfer.shape, F32),
            pltpu.VMEM(cluster_transfer.shape, F32),
            pltpu.VMEM(cluster_coupling.shape, F32),
            pltpu.VMEM((4 * LPD + 1, NVEC, 8, RANK), F32),
            pltpu.SemaphoreType.DMA((5 + LPD,)),
        ],
        compiler_params=params(12),
        cost_estimate=cost(40000000, 5000000),
        name="mid",
    )(
        *in_hbm(far_leaf, far_count, far_cluster),
        first,
        near,
        *in_hbm(
            leaf_transfer, cluster_transfer, bases, leaf_coupling, cluster_coupling, top_coupling
        ),
    )
    return pl.pallas_call(
        down_kernel,
        out_shape=sds(sources.shape, F32),
        in_specs=[SMEM] * 2 + [VMEM] * 7,
        out_specs=VMEM,
        scratch_shapes=[
            pltpu.VMEM((2 * LPD + 1, NVEC, 8, RANK), F32),
            pltpu.VMEM((8, WIDE), F32),
        ],
        compiler_params=params(8),
        name="down",
    )(
        *in_hbm(far_leaf, far_count),
        base,
        down_high,
        down_low,
        bases_v,
        coupling_v,
        top_v,
        second,
    )


def solution(mesh):
    placed = (
        P(None, ("grp", "dev")),
        P(("grp", "dev"), None, None),
        P(("grp", "dev"), None, None),
        P(("grp", "dev")),
        P(("grp", "dev"), None, None),
        P(("grp", "dev"), None),
        P(("grp", "dev")),
        P(("grp", "dev"), None, None, None),
        P(("grp", "dev"), None, None),
        P(("grp", "dev"), None),
        P(("grp", "dev"), None, None, None),
        P(("grp", "dev"), None, None),
        P("grp", None, None, None),
    )
    return jax.shard_map(
        per_device, mesh=mesh, in_specs=placed, out_specs=P(None, ("grp", "dev")), check_vma=False
    )
```

```python
import jax
import jax.numpy as jnp
from jax import lax
from jax.experimental import pallas as pl
from jax.experimental.pallas import tpu as pltpu
from jax.sharding import PartitionSpec as P

HIGH = lax.Precision.HIGHEST
F32 = jnp.float32
BF16 = jnp.bfloat16
LEAF = 512
RANK = 64
NVEC = 4
LPD = 4
FARW = 3
TURN = 31
WIDE = LPD * RANK
VMEM = pl.BlockSpec(memory_space=pltpu.VMEM)
HBM = pl.BlockSpec(memory_space=pltpu.HBM)
SMEM = pl.BlockSpec(memory_space=pltpu.SMEM)


def rows_by_rows(a, b, precision=None):
    return lax.dot_general(
        a, b, (((1,), (1,)), ((), ())), precision=precision, preferred_element_type=F32
    )


def exact_dot(a, b):
    return jnp.dot(a, b, precision=HIGH, preferred_element_type=F32)


def parts_of(rows):
    high = rows.astype(BF16).astype(F32)
    middle = (rows - high).astype(BF16).astype(F32)
    low = rows - high - middle
    return jnp.concatenate([high, middle, low, jnp.zeros_like(low)], axis=0).astype(BF16)


def two_parts(matrix):
    high = matrix.astype(BF16)
    return high, (matrix - high.astype(F32)).astype(BF16)


def close_dot(rows, matrix):
    parts = parts_of(rows)
    out = jnp.dot(parts, matrix[0], preferred_element_type=F32)
    small = jnp.dot(parts[:16], matrix[1], preferred_element_type=F32)
    return out[:8] + (out[8:16] + small[:8]) + (out[16:24] + small[8:16])


def tiles(matrix):
    return matrix.reshape(RANK // 8, 8, RANK)


def no_sums():
    return [jnp.zeros((RANK // 8, 8, RANK), F32) for _ in range(NVEC)]


def lanes_to_matrix(sums):
    lane = lax.broadcasted_iota(jnp.int32, (RANK, 128), 1)
    out = jnp.zeros((RANK, 128), F32)
    for v, s in enumerate(sums):
        column = jnp.sum(s, axis=-1, keepdims=True).reshape(RANK, 1)
        out = jnp.where(lane == v, column, out)
    return out


def spread(rows, v):
    return jnp.broadcast_to(rows[v : v + 1], (8, RANK))


def up_kernel(
    src_h, bases_h, leaf_h, cluster_h, send, src, bases, leaf, cluster, sem
):
    copies = [
        pltpu.make_async_copy(a, b, sem.at[i])
        for i, (a, b) in enumerate(
            (
                (leaf_h, leaf),
                (cluster_h, cluster),
                (src_h, src),
                (bases_h, bases),
            )
        )
    ]
    for c in copies:
        c.start()
    copies[0].wait()
    copies[1].wait()
    to_cluster = two_parts(leaf[...].reshape(WIDE, RANK))
    to_group = two_parts(cluster[0])
    copies[2].wait()
    copies[3].wait()
    every = jnp.concatenate(
        [rows_by_rows(src[:, l * LEAF : (l + 1) * LEAF], bases[l]) for l in range(LPD)], axis=1
    )
    cluster_rows = close_dot(jnp.concatenate([every, jnp.zeros_like(every)], axis=0), to_cluster)
    group_rows = close_dot(cluster_rows, to_group)
    row = jnp.concatenate([cluster_rows[:NVEC], group_rows[:NVEC], every], axis=1)
    for i in range(send.shape[0]):
        send[i] = row


def own_kernel(src, self_h, other_h, own, other, block, sem):
    copies = [
        pltpu.make_async_copy(self_h.at[l], block.at[l], sem.at[l]) for l in range(LPD)
    ] + [pltpu.make_async_copy(other_h, other, sem.at[LPD])]
    for c in copies:
        c.start()
    for l in range(LPD):
        at = slice(l * LEAF, (l + 1) * LEAF)
        copies[l].wait()
        own[:, at] = rows_by_rows(src[:, at], block[l])
    copies[LPD].wait()


def near_kernel(near_list, src, even_swap, odd_swap, own, other, near):
    me = lax.axis_index("grp") * lax.axis_size("dev") + lax.axis_index("dev")
    is_odd = (me & 1) == 1
    for l in range(LPD):
        here = jnp.clip(near_list[l] - me * LPD + LPD, 0, 3 * LPD - 1)
        at = pl.multiple_of((here & (LPD - 1)) * LEAF, LEAF)
        which = here >> 2
        x1 = src[:, pl.ds(at, LEAF)]
        x2 = odd_swap[:, pl.ds(at, LEAF)]
        x3 = even_swap[:, pl.ds(at, LEAF)]
        x = jnp.where(which == 1, x1, jnp.where((which == 0) == is_odd, x2, x3))
        at = slice(l * LEAF, (l + 1) * LEAF)
        near[:, at] = own[:, at] + rows_by_rows(x, other[l])


def group_kernel(first, send):
    d = lax.axis_index("dev")
    n_dev = first.shape[0]
    total = jnp.sum(first[:, :, : 2 * RANK], axis=0)
    low = d < FARW
    a = jnp.where(low, jnp.minimum(n_dev - FARW + d, n_dev - 1), jnp.maximum(d - (n_dev - 2), 0))
    b = jnp.where(
        low, jnp.minimum(n_dev - FARW + 1 + d, n_dev - 1), jnp.maximum(d - (n_dev - FARW), 0)
    )
    a, b = (a - TURN) & (n_dev - 1), (b - TURN) & (n_dev - 1)
    row = jnp.concatenate([total, first[a, :, 2 * RANK :], first[b, :, 2 * RANK :]], axis=1)
    for i in range(send.shape[0]):
        send[i] = row


def far_sums(coupling, l, table, entry):
    sums = no_sums()
    for s in range(coupling.shape[1]):
        c = tiles(coupling[l, s])
        at = entry(l, s)
        for v in range(NVEC):
            sums[v] = sums[v] + c * table[at, v][None]
    return lanes_to_matrix(sums)


def fill(table, first_entry, value):
    for l in range(LPD):
        for v in range(NVEC):
            table[first_entry + l, v] = spread(value[:, l * RANK : (l + 1) * RANK], v)


def mid_kernel(
    far_leaf, far_count, far_cluster, first, near, leaf_h, transfer_h, bases_h, coupling_h,
    cluster_h, top_h, base, down_high, down_low, bases, coupling, top_out, leaf_transfer, transfer,
    cluster, table, sem
):
    copies = []
    for a, b in (
        [(leaf_h, leaf_transfer), (transfer_h, transfer), (cluster_h, cluster)]
        + [(bases_h, bases)]
        + [(coupling_h.at[l], coupling.at[l]) for l in range(LPD)]
        + [(top_h, top_out)]
    ):
        copy = pltpu.make_async_copy(a, b, sem.at[len(copies)])
        copy.start()
        copies.append(copy)
    d = lax.axis_index("dev")
    n_dev = lax.axis_size("dev")
    me = lax.axis_index("grp") * n_dev + d

    for pos, off in enumerate((-3, -2, 2, 3)):
        fill(table, pos * LPD, first[(d + off - TURN) & (n_dev - 1), :, 2 * RANK :])
    table[4 * LPD] = jnp.zeros((NVEC, 8, RANK), F32)

    for c in copies[:3]:
        c.wait()
    to_cluster = leaf_transfer[...].reshape(WIDE, RANK)
    to_group = exact_dot(to_cluster, transfer[0])
    high = to_group.astype(BF16)
    down_high[...] = high
    down_low[...] = (to_group - high.astype(F32)).astype(BF16)
    sums = no_sums()
    for s in range(far_cluster.shape[1]):
        c = tiles(cluster[0, s])
        x = first[(far_cluster[0, s] - TURN) & (n_dev - 1), :, :RANK]
        for v in range(NVEC):
            sums[v] = sums[v] + c * spread(x, v)[None]
    from_cluster = exact_dot(to_cluster, lanes_to_matrix(sums))

    def entry(l, s):
        leaf = far_leaf[l, s]
        delta = (leaf >> 2) - me
        pos = jnp.where(delta < 0, delta + FARW, delta)
        here = jnp.logical_and(d + delta >= 0, d + delta < n_dev)
        live = jnp.logical_and(s < far_count[l], here)
        return jnp.clip(jnp.where(live, pos * LPD + (leaf & (LPD - 1)), 4 * LPD), 0, 4 * LPD)

    copies[3].wait()
    for l in range(LPD):
        copies[4 + l].wait()
        field = far_sums(coupling, l, table, entry) + from_cluster[l * RANK : (l + 1) * RANK]
        product = jnp.dot(
            parts_of(jnp.transpose(field)[:8]), bases[l], preferred_element_type=F32
        )
        product = product[:8] + product[8:16] + product[16:24]
        at = slice(l * LEAF, (l + 1) * LEAF)
        base[:, at] = near[:, at] + product[:NVEC]
    copies[4 + LPD].wait()


def down_kernel(
    far_leaf, far_count, base, down_high, down_low, bases, coupling, top_coupling, second, out,
    table
):
    g = lax.axis_index("grp")
    d = lax.axis_index("dev")
    n_dev = lax.axis_size("dev")
    n_grp = second.shape[0]
    me = g * n_dev + d

    sums = no_sums()
    for h in range(n_grp):
        c = tiles(top_coupling[0, h])
        x = jnp.where(h != g, second[h, :, RANK : 2 * RANK], 0.0)
        for v in range(NVEC):
            sums[v] = sums[v] + c * spread(x, v)[None]
    parts = parts_of(jnp.transpose(lanes_to_matrix(sums))[:8])
    field = rows_by_rows(parts, down_high[...])
    field = field[:8] + field[8:16] + field[16:24] + rows_by_rows(parts[:16], down_low[...])[:8]

    side = (g + jnp.where(d < FARW, -1, 1)) & (n_grp - 1)
    for k in range(2):
        start = 2 * RANK + k * WIDE
        fill(table, k * LPD, second[side, :, start : start + WIDE])
    table[2 * LPD] = jnp.zeros((NVEC, 8, RANK), F32)

    def entry(l, s):
        leaf = far_leaf[l, s]
        delta = (leaf >> 2) - me
        which = jnp.where(delta < 0, delta + FARW, delta) & 1
        there = jnp.logical_or(d + delta < 0, d + delta >= n_dev)
        live = jnp.logical_and(s < far_count[l], there)
        return jnp.where(live, which * LPD + (leaf & (LPD - 1)), 2 * LPD)

    for l in range(LPD):
        extra = jnp.transpose(far_sums(coupling, l, table, entry))[:8]
        parts = parts_of(field[:, l * RANK : (l + 1) * RANK] + extra)
        far = jnp.dot(parts, bases[l], preferred_element_type=F32)
        far = far[:8] + far[8:16] + far[16:24]
        at = slice(l * LEAF, (l + 1) * LEAF)
        out[:, at] = base[:, at] + far[:NVEC]


def permute(value, pairs):
    return lax.ppermute(value, ("grp", "dev"), pairs)


def swapped(value, start, count):
    pairs = [(i, (i + 1) % count) for i in range(start, count, 2)]
    return lax.ppermute(value, ("grp", "dev"), pairs + [(j, i) for i, j in pairs])


def in_hbm(*arrays):
    return [pltpu.with_memory_space_constraint(a, pltpu.HBM) for a in arrays]


def params(mib):
    return pltpu.CompilerParams(vmem_limit_bytes=mib * 1024 * 1024)


def cost(flops, size):
    return pl.CostEstimate(flops=flops, bytes_accessed=size, transcendentals=0)


def per_device(
    sources,
    self_near_block,
    neighbour_near_block,
    near_list,
    bases,
    far_leaf,
    far_count,
    leaf_coupling,
    leaf_transfer,
    far_cluster,
    cluster_coupling,
    cluster_transfer,
    top_coupling,
):
    n_dev = lax.axis_size("dev")
    n_grp = lax.axis_size("grp")
    n_all = n_dev * n_grp
    sds = jax.ShapeDtypeStruct
    send = pl.pallas_call(
        up_kernel,
        out_shape=sds((n_dev, NVEC, 2 * RANK + WIDE), F32),
        in_specs=[HBM] * 4,
        out_specs=VMEM,
        scratch_shapes=[
            pltpu.VMEM(sources.shape, BF16),
            pltpu.VMEM(bases.shape, BF16),
            pltpu.VMEM(leaf_transfer.shape, F32),
            pltpu.VMEM(cluster_transfer.shape, F32),
            pltpu.SemaphoreType.DMA((4,)),
        ],
        compiler_params=params(8),
        name="up",
    )(*in_hbm(sources, bases, leaf_transfer, cluster_transfer))
    turned = [(i + TURN) % n_dev for i in range(n_dev)]
    first = lax.all_to_all(send, "dev", 0, 0, axis_index_groups=[turned])
    send, tied = lax.optimization_barrier((send, sources))
    even_swap = swapped(tied, 1, n_all)
    odd_swap = swapped(tied, 0, n_all)
    own, other_v = pl.pallas_call(
        own_kernel,
        out_shape=[sds(sources.shape, F32), sds(neighbour_near_block.shape, BF16)],
        in_specs=[VMEM] + [HBM] * 2,
        out_specs=[VMEM] * 2,
        scratch_shapes=[
            pltpu.VMEM(self_near_block.shape, BF16),
            pltpu.SemaphoreType.DMA((1 + LPD,)),
        ],
        compiler_params=params(8),
        cost_estimate=cost(20000000, 4000000),
        name="own",
    )(*in_hbm(tied, self_near_block, neighbour_near_block))
    near = pl.pallas_call(
        near_kernel,
        out_shape=sds(sources.shape, F32),
        in_specs=[SMEM] + [VMEM] * 5,
        out_specs=VMEM,
        compiler_params=params(4),
        cost_estimate=cost(20000000, 2000000),
        name="near",
    )(*in_hbm(near_list, tied), even_swap, odd_swap, own, other_v)
    first, near = lax.optimization_barrier((first, near))
    send = pl.pallas_call(
        group_kernel,
        out_shape=sds((n_grp, NVEC, 2 * RANK + 2 * WIDE), F32),
        in_specs=[VMEM],
        out_specs=VMEM,
        compiler_params=params(4),
        name="group",
    )(first)
    second = lax.all_to_all(send, "grp", 0, 0)
    base, down_high, down_low, bases_v, coupling_v, top_v = pl.pallas_call(
        mid_kernel,
        out_shape=[
            sds(sources.shape, F32),
            sds((WIDE, RANK), BF16),
            sds((WIDE, RANK), BF16),
            sds(bases.shape, BF16),
            sds(leaf_coupling.shape, F32),
            sds(top_coupling.shape, F32),
        ],
        in_specs=[SMEM] * 3 + [VMEM] * 2 + [HBM] * 6,
        out_specs=[VMEM] * 6,
        scratch_shapes=[
            pltpu.VMEM(leaf_transfer.shape, F32),
            pltpu.VMEM(cluster_transfer.shape, F32),
            pltpu.VMEM(cluster_coupling.shape, F32),
            pltpu.VMEM((4 * LPD + 1, NVEC, 8, RANK), F32),
            pltpu.SemaphoreType.DMA((5 + LPD,)),
        ],
        compiler_params=params(12),
        cost_estimate=cost(40000000, 5000000),
        name="mid",
    )(
        *in_hbm(far_leaf, far_count, far_cluster),
        first,
        near,
        *in_hbm(
            leaf_transfer, cluster_transfer, bases, leaf_coupling, cluster_coupling, top_coupling
        ),
    )
    return pl.pallas_call(
        down_kernel,
        out_shape=sds(sources.shape, F32),
        in_specs=[SMEM] * 2 + [VMEM] * 7,
        out_specs=VMEM,
        scratch_shapes=[
            pltpu.VMEM((2 * LPD + 1, NVEC, 8, RANK), F32),
        ],
        compiler_params=params(8),
        name="down",
    )(
        *in_hbm(far_leaf, far_count),
        base,
        down_high,
        down_low,
        bases_v,
        coupling_v,
        top_v,
        second,
    )


def solution(mesh):
    placed = (
        P(None, ("grp", "dev")),
        P(("grp", "dev"), None, None),
        P(("grp", "dev"), None, None),
        P(("grp", "dev")),
        P(("grp", "dev"), None, None),
        P(("grp", "dev"), None),
        P(("grp", "dev")),
        P(("grp", "dev"), None, None, None),
        P(("grp", "dev"), None, None),
        P(("grp", "dev"), None),
        P(("grp", "dev"), None, None, None),
        P(("grp", "dev"), None, None),
        P("grp", None, None, None),
    )
    return jax.shard_map(
        per_device, mesh=mesh, in_specs=placed, out_specs=P(None, ("grp", "dev")), check_vma=False
    )
```

```python
import jax
import jax.numpy as jnp
from jax import lax
from jax.experimental import pallas as pl
from jax.experimental.pallas import tpu as pltpu
from jax.sharding import PartitionSpec as P

HIGH = lax.Precision.HIGHEST
F32 = jnp.float32
BF16 = jnp.bfloat16
LEAF = 512
RANK = 64
NVEC = 4
LPD = 4
FARW = 3
GRP_TURN = 2
TURN = 31
WIDE = LPD * RANK
VMEM = pl.BlockSpec(memory_space=pltpu.VMEM)
HBM = pl.BlockSpec(memory_space=pltpu.HBM)
SMEM = pl.BlockSpec(memory_space=pltpu.SMEM)


def rows_by_rows(a, b, precision=None):
    return lax.dot_general(
        a, b, (((1,), (1,)), ((), ())), precision=precision, preferred_element_type=F32
    )


def exact_dot(a, b):
    return jnp.dot(a, b, precision=HIGH, preferred_element_type=F32)


def parts_of(rows):
    high = rows.astype(BF16).astype(F32)
    middle = (rows - high).astype(BF16).astype(F32)
    low = rows - high - middle
    return jnp.concatenate([high, middle, low, jnp.zeros_like(low)], axis=0).astype(BF16)


def two_parts(matrix):
    high = matrix.astype(BF16)
    return high, (matrix - high.astype(F32)).astype(BF16)


def close_dot(rows, matrix):
    parts = parts_of(rows)
    out = jnp.dot(parts, matrix[0], preferred_element_type=F32)
    small = jnp.dot(parts[:16], matrix[1], preferred_element_type=F32)
    return out[:8] + (out[8:16] + small[:8]) + (out[16:24] + small[8:16])


def tiles(matrix):
    return matrix.reshape(RANK // 8, 8, RANK)


def no_sums():
    return [jnp.zeros((RANK // 8, 8, RANK), F32) for _ in range(NVEC)]


def lanes_to_matrix(sums):
    lane = lax.broadcasted_iota(jnp.int32, (RANK, 128), 1)
    out = jnp.zeros((RANK, 128), F32)
    for v, s in enumerate(sums):
        column = jnp.sum(s, axis=-1, keepdims=True).reshape(RANK, 1)
        out = jnp.where(lane == v, column, out)
    return out


def spread(rows, v):
    return jnp.broadcast_to(rows[v : v + 1], (8, RANK))


def up_kernel(
    src_h, bases_h, leaf_h, cluster_h, send, src, bases, leaf, cluster, sem
):
    copies = [
        pltpu.make_async_copy(a, b, sem.at[i])
        for i, (a, b) in enumerate(
            (
                (src_h, src),
                (bases_h, bases),
                (leaf_h, leaf),
                (cluster_h, cluster),
            )
        )
    ]
    for c in copies:
        c.start()
    copies[0].wait()
    copies[1].wait()
    every = jnp.concatenate(
        [rows_by_rows(src[:, l * LEAF : (l + 1) * LEAF], bases[l]) for l in range(LPD)], axis=1
    )
    copies[2].wait()
    to_cluster = two_parts(leaf[...].reshape(WIDE, RANK))
    copies[3].wait()
    to_group = two_parts(cluster[0])
    cluster_rows = close_dot(jnp.concatenate([every, jnp.zeros_like(every)], axis=0), to_cluster)
    group_rows = close_dot(cluster_rows, to_group)
    row = jnp.concatenate([cluster_rows[:NVEC], group_rows[:NVEC], every], axis=1)
    for i in range(send.shape[0]):
        send[i] = row


def own_kernel(src, self_h, other_h, own, other, block, sem):
    copies = [
        pltpu.make_async_copy(self_h.at[l], block.at[l], sem.at[l]) for l in range(LPD)
    ] + [pltpu.make_async_copy(other_h, other, sem.at[LPD])]
    for c in copies:
        c.start()
    for l in range(LPD):
        at = slice(l * LEAF, (l + 1) * LEAF)
        copies[l].wait()
        own[:, at] = rows_by_rows(src[:, at], block[l])
    copies[LPD].wait()


def near_kernel(near_list, src, even_swap, odd_swap, own, other, near):
    me = lax.axis_index("grp") * lax.axis_size("dev") + lax.axis_index("dev")
    is_odd = (me & 1) == 1
    for l in range(LPD):
        here = jnp.clip(near_list[l] - me * LPD + LPD, 0, 3 * LPD - 1)
        at = pl.multiple_of((here & (LPD - 1)) * LEAF, LEAF)
        which = here >> 2
        x1 = src[:, pl.ds(at, LEAF)]
        x2 = odd_swap[:, pl.ds(at, LEAF)]
        x3 = even_swap[:, pl.ds(at, LEAF)]
        x = jnp.where(which == 1, x1, jnp.where((which == 0) == is_odd, x2, x3))
        at = slice(l * LEAF, (l + 1) * LEAF)
        near[:, at] = own[:, at] + rows_by_rows(x, other[l])


def group_kernel(first, send):
    d = lax.axis_index("dev")
    n_dev = first.shape[0]
    total = jnp.sum(first[:, :, : 2 * RANK], axis=0)
    low = d < FARW
    a = jnp.where(low, jnp.minimum(n_dev - FARW + d, n_dev - 1), jnp.maximum(d - (n_dev - 2), 0))
    b = jnp.where(
        low, jnp.minimum(n_dev - FARW + 1 + d, n_dev - 1), jnp.maximum(d - (n_dev - FARW), 0)
    )
    a, b = (a - TURN) & (n_dev - 1), (b - TURN) & (n_dev - 1)
    row = jnp.concatenate([total, first[a, :, 2 * RANK :], first[b, :, 2 * RANK :]], axis=1)
    for i in range(send.shape[0]):
        send[i] = row


def far_sums(coupling, l, table, entry):
    sums = no_sums()
    for s in range(coupling.shape[1]):
        c = tiles(coupling[l, s])
        at = entry(l, s)
        for v in range(NVEC):
            sums[v] = sums[v] + c * table[at, v][None]
    return lanes_to_matrix(sums)


def fill(table, first_entry, value):
    for l in range(LPD):
        for v in range(NVEC):
            table[first_entry + l, v] = spread(value[:, l * RANK : (l + 1) * RANK], v)


def mid_kernel(
    far_leaf, far_count, far_cluster, first, near, leaf_h, transfer_h, bases_h, coupling_h,
    cluster_h, top_h, base, down_high, down_low, bases, coupling, top_out, leaf_transfer, transfer,
    cluster, table, sem
):
    copies = []
    for a, b in (
        [(leaf_h, leaf_transfer), (transfer_h, transfer), (cluster_h, cluster)]
        + [(bases_h, bases)]
        + [(coupling_h.at[l], coupling.at[l]) for l in range(LPD)]
        + [(top_h, top_out)]
    ):
        copy = pltpu.make_async_copy(a, b, sem.at[len(copies)])
        copy.start()
        copies.append(copy)
    d = lax.axis_index("dev")
    n_dev = lax.axis_size("dev")
    me = lax.axis_index("grp") * n_dev + d

    for pos, off in enumerate((-3, -2, 2, 3)):
        fill(table, pos * LPD, first[(d + off - TURN) & (n_dev - 1), :, 2 * RANK :])
    table[4 * LPD] = jnp.zeros((NVEC, 8, RANK), F32)

    for c in copies[:3]:
        c.wait()
    to_cluster = leaf_transfer[...].reshape(WIDE, RANK)
    to_group = exact_dot(to_cluster, transfer[0])
    high = to_group.astype(BF16)
    down_high[...] = high
    down_low[...] = (to_group - high.astype(F32)).astype(BF16)
    sums = no_sums()
    for s in range(far_cluster.shape[1]):
        c = tiles(cluster[0, s])
        x = first[(far_cluster[0, s] - TURN) & (n_dev - 1), :, :RANK]
        for v in range(NVEC):
            sums[v] = sums[v] + c * spread(x, v)[None]
    from_cluster = exact_dot(to_cluster, lanes_to_matrix(sums))

    def entry(l, s):
        leaf = far_leaf[l, s]
        delta = (leaf >> 2) - me
        pos = jnp.where(delta < 0, delta + FARW, delta)
        here = jnp.logical_and(d + delta >= 0, d + delta < n_dev)
        live = jnp.logical_and(s < far_count[l], here)
        return jnp.clip(jnp.where(live, pos * LPD + (leaf & (LPD - 1)), 4 * LPD), 0, 4 * LPD)

    copies[3].wait()
    for l in range(LPD):
        copies[4 + l].wait()
        field = far_sums(coupling, l, table, entry) + from_cluster[l * RANK : (l + 1) * RANK]
        product = jnp.dot(
            parts_of(jnp.transpose(field)[:8]), bases[l], preferred_element_type=F32
        )
        product = product[:8] + product[8:16] + product[16:24]
        at = slice(l * LEAF, (l + 1) * LEAF)
        base[:, at] = near[:, at] + product[:NVEC]
    copies[4 + LPD].wait()


def down_kernel(
    far_leaf, far_count, base, down_high, down_low, bases, coupling, top_coupling, second, out,
    table
):
    g = lax.axis_index("grp")
    d = lax.axis_index("dev")
    n_dev = lax.axis_size("dev")
    n_grp = second.shape[0]
    me = g * n_dev + d

    sums = no_sums()
    for h in range(n_grp):
        c = tiles(top_coupling[0, h])
        x = second[(h - GRP_TURN) % n_grp, :, RANK : 2 * RANK]
        x = jnp.where(h != g, x, 0.0)
        for v in range(NVEC):
            sums[v] = sums[v] + c * spread(x, v)[None]
    parts = parts_of(jnp.transpose(lanes_to_matrix(sums))[:8])
    field = rows_by_rows(parts, down_high[...])
    field = field[:8] + field[8:16] + field[16:24] + rows_by_rows(parts[:16], down_low[...])[:8]

    side = (g + jnp.where(d < FARW, -1, 1) - GRP_TURN) & (n_grp - 1)
    for k in range(2):
        start = 2 * RANK + k * WIDE
        fill(table, k * LPD, second[side, :, start : start + WIDE])
    table[2 * LPD] = jnp.zeros((NVEC, 8, RANK), F32)

    def entry(l, s):
        leaf = far_leaf[l, s]
        delta = (leaf >> 2) - me
        which = jnp.where(delta < 0, delta + FARW, delta) & 1
        there = jnp.logical_or(d + delta < 0, d + delta >= n_dev)
        live = jnp.logical_and(s < far_count[l], there)
        return jnp.where(live, which * LPD + (leaf & (LPD - 1)), 2 * LPD)

    for l in range(LPD):
        extra = jnp.transpose(far_sums(coupling, l, table, entry))[:8]
        parts = parts_of(field[:, l * RANK : (l + 1) * RANK] + extra)
        far = jnp.dot(parts, bases[l], preferred_element_type=F32)
        far = far[:8] + far[8:16] + far[16:24]
        at = slice(l * LEAF, (l + 1) * LEAF)
        out[:, at] = base[:, at] + far[:NVEC]


def permute(value, pairs):
    return lax.ppermute(value, ("grp", "dev"), pairs)


def swapped(value, start, count):
    pairs = [(i, (i + 1) % count) for i in range(start, count, 2)]
    return lax.ppermute(value, ("grp", "dev"), pairs + [(j, i) for i, j in pairs])


def in_hbm(*arrays):
    return [pltpu.with_memory_space_constraint(a, pltpu.HBM) for a in arrays]


def params(mib):
    return pltpu.CompilerParams(vmem_limit_bytes=mib * 1024 * 1024)


def cost(flops, size):
    return pl.CostEstimate(flops=flops, bytes_accessed=size, transcendentals=0)


def per_device(
    sources,
    self_near_block,
    neighbour_near_block,
    near_list,
    bases,
    far_leaf,
    far_count,
    leaf_coupling,
    leaf_transfer,
    far_cluster,
    cluster_coupling,
    cluster_transfer,
    top_coupling,
):
    n_dev = lax.axis_size("dev")
    n_grp = lax.axis_size("grp")
    n_all = n_dev * n_grp
    sds = jax.ShapeDtypeStruct
    send = pl.pallas_call(
        up_kernel,
        out_shape=sds((n_dev, NVEC, 2 * RANK + WIDE), F32),
        in_specs=[HBM] * 4,
        out_specs=VMEM,
        scratch_shapes=[
            pltpu.VMEM(sources.shape, BF16),
            pltpu.VMEM(bases.shape, BF16),
            pltpu.VMEM(leaf_transfer.shape, F32),
            pltpu.VMEM(cluster_transfer.shape, F32),
            pltpu.SemaphoreType.DMA((4,)),
        ],
        compiler_params=params(8),
        name="up",
    )(*in_hbm(sources, bases, leaf_transfer, cluster_transfer))
    turned = [(i + TURN) % n_dev for i in range(n_dev)]
    first = lax.all_to_all(send, "dev", 0, 0, axis_index_groups=[turned])
    send, tied = lax.optimization_barrier((send, sources))
    even_swap = swapped(tied, 1, n_all)
    odd_swap = swapped(tied, 0, n_all)
    own, other_v = pl.pallas_call(
        own_kernel,
        out_shape=[sds(sources.shape, F32), sds(neighbour_near_block.shape, BF16)],
        in_specs=[VMEM] + [HBM] * 2,
        out_specs=[VMEM] * 2,
        scratch_shapes=[
            pltpu.VMEM(self_near_block.shape, BF16),
            pltpu.SemaphoreType.DMA((1 + LPD,)),
        ],
        compiler_params=params(8),
        cost_estimate=cost(20000000, 4000000),
        name="own",
    )(*in_hbm(tied, self_near_block, neighbour_near_block))
    near = pl.pallas_call(
        near_kernel,
        out_shape=sds(sources.shape, F32),
        in_specs=[SMEM] + [VMEM] * 5,
        out_specs=VMEM,
        compiler_params=params(4),
        cost_estimate=cost(20000000, 2000000),
        name="near",
    )(*in_hbm(near_list, tied), even_swap, odd_swap, own, other_v)
    first, near = lax.optimization_barrier((first, near))
    send = pl.pallas_call(
        group_kernel,
        out_shape=sds((n_grp, NVEC, 2 * RANK + 2 * WIDE), F32),
        in_specs=[VMEM],
        out_specs=VMEM,
        compiler_params=params(4),
        name="group",
    )(first)
    turned = [(i + GRP_TURN) % n_grp for i in range(n_grp)]
    second = lax.all_to_all(send, "grp", 0, 0, axis_index_groups=[turned])
    base, down_high, down_low, bases_v, coupling_v, top_v = pl.pallas_call(
        mid_kernel,
        out_shape=[
            sds(sources.shape, F32),
            sds((WIDE, RANK), BF16),
            sds((WIDE, RANK), BF16),
            sds(bases.shape, BF16),
            sds(leaf_coupling.shape, F32),
            sds(top_coupling.shape, F32),
        ],
        in_specs=[SMEM] * 3 + [VMEM] * 2 + [HBM] * 6,
        out_specs=[VMEM] * 6,
        scratch_shapes=[
            pltpu.VMEM(leaf_transfer.shape, F32),
            pltpu.VMEM(cluster_transfer.shape, F32),
            pltpu.VMEM(cluster_coupling.shape, F32),
            pltpu.VMEM((4 * LPD + 1, NVEC, 8, RANK), F32),
            pltpu.SemaphoreType.DMA((5 + LPD,)),
        ],
        compiler_params=params(12),
        cost_estimate=cost(40000000, 5000000),
        name="mid",
    )(
        *in_hbm(far_leaf, far_count, far_cluster),
        first,
        near,
        *in_hbm(
            leaf_transfer, cluster_transfer, bases, leaf_coupling, cluster_coupling, top_coupling
        ),
    )
    return pl.pallas_call(
        down_kernel,
        out_shape=sds(sources.shape, F32),
        in_specs=[SMEM] * 2 + [VMEM] * 7,
        out_specs=VMEM,
        scratch_shapes=[
            pltpu.VMEM((2 * LPD + 1, NVEC, 8, RANK), F32),
        ],
        compiler_params=params(8),
        name="down",
    )(
        *in_hbm(far_leaf, far_count),
        base,
        down_high,
        down_low,
        bases_v,
        coupling_v,
        top_v,
        second,
    )


def solution(mesh):
    placed = (
        P(None, ("grp", "dev")),
        P(("grp", "dev"), None, None),
        P(("grp", "dev"), None, None),
        P(("grp", "dev")),
        P(("grp", "dev"), None, None),
        P(("grp", "dev"), None),
        P(("grp", "dev")),
        P(("grp", "dev"), None, None, None),
        P(("grp", "dev"), None, None),
        P(("grp", "dev"), None),
        P(("grp", "dev"), None, None, None),
        P(("grp", "dev"), None, None),
        P("grp", None, None, None),
    )
    return jax.shard_map(
        per_device, mesh=mesh, in_specs=placed, out_specs=P(None, ("grp", "dev")), check_vma=False
    )
```

```python
import jax
import jax.numpy as jnp
from jax import lax
from jax.experimental import pallas as pl
from jax.experimental.pallas import tpu as pltpu
from jax.sharding import PartitionSpec as P

HIGH = lax.Precision.HIGHEST
F32 = jnp.float32
BF16 = jnp.bfloat16
LEAF = 512
RANK = 64
NVEC = 4
LPD = 4
FARW = 3
GRP_TURN = 3
TURN = 15
WIDE = LPD * RANK
VMEM = pl.BlockSpec(memory_space=pltpu.VMEM)
HBM = pl.BlockSpec(memory_space=pltpu.HBM)
SMEM = pl.BlockSpec(memory_space=pltpu.SMEM)


def rows_by_rows(a, b, precision=None):
    return lax.dot_general(
        a, b, (((1,), (1,)), ((), ())), precision=precision, preferred_element_type=F32
    )


def split_dot(a, b):
    a_high, a_low = two_parts(a)
    b_high, b_low = two_parts(b)
    return (
        jnp.dot(a_high, b_high, preferred_element_type=F32)
        + jnp.dot(a_high, b_low, preferred_element_type=F32)
        + jnp.dot(a_low, b_high, preferred_element_type=F32)
    )


def parts_of(rows):
    high = rows.astype(BF16).astype(F32)
    middle = (rows - high).astype(BF16).astype(F32)
    low = rows - high - middle
    return jnp.concatenate([high, middle, low, jnp.zeros_like(low)], axis=0).astype(BF16)


def two_parts(matrix):
    high = matrix.astype(BF16)
    return high, (matrix - high.astype(F32)).astype(BF16)


def close_dot(rows, matrix):
    parts = parts_of(rows)
    out = jnp.dot(parts, matrix[0], preferred_element_type=F32)
    small = jnp.dot(parts[:16], matrix[1], preferred_element_type=F32)
    return out[:8] + (out[8:16] + small[:8]) + (out[16:24] + small[8:16])


def tiles(matrix):
    return matrix.reshape(RANK // 8, 8, RANK)


def no_sums():
    return [jnp.zeros((RANK // 8, 8, RANK), F32) for _ in range(NVEC)]


def lanes_to_matrix(sums):
    lane = lax.broadcasted_iota(jnp.int32, (RANK, 128), 1)
    out = jnp.zeros((RANK, 128), F32)
    for v, s in enumerate(sums):
        column = jnp.sum(s, axis=-1, keepdims=True).reshape(RANK, 1)
        out = jnp.where(lane == v, column, out)
    return out


def spread(rows, v):
    return jnp.broadcast_to(rows[v : v + 1], (8, RANK))


def up_kernel(
    src_h, bases_h, leaf_h, cluster_h, send, src, bases, leaf, cluster, sem
):
    copies = [
        pltpu.make_async_copy(a, b, sem.at[i])
        for i, (a, b) in enumerate(
            (
                (src_h, src),
                (bases_h, bases),
                (leaf_h, leaf),
                (cluster_h, cluster),
            )
        )
    ]
    for c in copies:
        c.start()
    copies[0].wait()
    copies[1].wait()
    every = jnp.concatenate(
        [rows_by_rows(src[:, l * LEAF : (l + 1) * LEAF], bases[l]) for l in range(LPD)], axis=1
    )
    copies[2].wait()
    to_cluster = two_parts(leaf[...].reshape(WIDE, RANK))
    copies[3].wait()
    to_group = two_parts(cluster[0])
    cluster_rows = close_dot(jnp.concatenate([every, jnp.zeros_like(every)], axis=0), to_cluster)
    group_rows = close_dot(cluster_rows, to_group)
    row = jnp.concatenate([cluster_rows[:NVEC], group_rows[:NVEC], every], axis=1)
    for i in range(send.shape[0]):
        send[i] = row


def own_kernel(src, self_h, other_h, own, other, block, sem):
    copies = [
        pltpu.make_async_copy(self_h.at[l], block.at[l], sem.at[l]) for l in range(LPD)
    ] + [pltpu.make_async_copy(other_h, other, sem.at[LPD])]
    for c in copies:
        c.start()
    for l in range(LPD):
        at = slice(l * LEAF, (l + 1) * LEAF)
        copies[l].wait()
        own[:, at] = rows_by_rows(src[:, at], block[l])
    copies[LPD].wait()


def near_kernel(near_list, src, even_swap, odd_swap, own, other, near):
    me = lax.axis_index("grp") * lax.axis_size("dev") + lax.axis_index("dev")
    is_odd = (me & 1) == 1
    for l in range(LPD):
        here = jnp.clip(near_list[l] - me * LPD + LPD, 0, 3 * LPD - 1)
        at = pl.multiple_of((here & (LPD - 1)) * LEAF, LEAF)
        which = here >> 2
        x1 = src[:, pl.ds(at, LEAF)]
        x2 = odd_swap[:, pl.ds(at, LEAF)]
        x3 = even_swap[:, pl.ds(at, LEAF)]
        x = jnp.where(which == 1, x1, jnp.where((which == 0) == is_odd, x2, x3))
        at = slice(l * LEAF, (l + 1) * LEAF)
        near[:, at] = own[:, at] + rows_by_rows(x, other[l])


def group_kernel(first, send):
    d = lax.axis_index("dev")
    n_dev = first.shape[0]
    total = jnp.sum(first[:, :, : 2 * RANK], axis=0)
    low = d < FARW
    a = jnp.where(low, jnp.minimum(n_dev - FARW + d, n_dev - 1), jnp.maximum(d - (n_dev - 2), 0))
    b = jnp.where(
        low, jnp.minimum(n_dev - FARW + 1 + d, n_dev - 1), jnp.maximum(d - (n_dev - FARW), 0)
    )
    a, b = (a - TURN) & (n_dev - 1), (b - TURN) & (n_dev - 1)
    row = jnp.concatenate([total, first[a, :, 2 * RANK :], first[b, :, 2 * RANK :]], axis=1)
    for i in range(send.shape[0]):
        send[i] = row


def far_sums(coupling, l, table, entry):
    sums = no_sums()
    for s in range(coupling.shape[1]):
        c = tiles(coupling[l, s])
        at = entry(l, s)
        for v in range(NVEC):
            sums[v] = sums[v] + c * table[at, v][None]
    return lanes_to_matrix(sums)


def fill(table, first_entry, value):
    for l in range(LPD):
        for v in range(NVEC):
            table[first_entry + l, v] = spread(value[:, l * RANK : (l + 1) * RANK], v)


def mid_kernel(
    far_leaf, far_count, far_cluster, first, near, leaf_h, transfer_h, bases_h, coupling_h,
    cluster_h, top_h, base, down_high, down_low, bases, coupling, top_out, leaf_transfer, transfer,
    cluster, table, sem
):
    copies = []
    for a, b in (
        [(leaf_h, leaf_transfer), (transfer_h, transfer), (cluster_h, cluster)]
        + [(bases_h, bases)]
        + [(coupling_h.at[l], coupling.at[l]) for l in range(LPD)]
        + [(top_h, top_out)]
    ):
        copy = pltpu.make_async_copy(a, b, sem.at[len(copies)])
        copy.start()
        copies.append(copy)
    d = lax.axis_index("dev")
    n_dev = lax.axis_size("dev")
    me = lax.axis_index("grp") * n_dev + d

    for pos, off in enumerate((-3, -2, 2, 3)):
        fill(table, pos * LPD, first[(d + off - TURN) & (n_dev - 1), :, 2 * RANK :])
    table[4 * LPD] = jnp.zeros((NVEC, 8, RANK), F32)

    for c in copies[:3]:
        c.wait()
    to_cluster = leaf_transfer[...].reshape(WIDE, RANK)
    to_group = split_dot(to_cluster, transfer[0])
    high = to_group.astype(BF16)
    down_high[...] = high
    down_low[...] = (to_group - high.astype(F32)).astype(BF16)
    sums = no_sums()
    for s in range(far_cluster.shape[1]):
        c = tiles(cluster[0, s])
        x = first[(far_cluster[0, s] - TURN) & (n_dev - 1), :, :RANK]
        for v in range(NVEC):
            sums[v] = sums[v] + c * spread(x, v)[None]
    from_cluster = split_dot(to_cluster, lanes_to_matrix(sums))

    def entry(l, s):
        leaf = far_leaf[l, s]
        delta = (leaf >> 2) - me
        pos = jnp.where(delta < 0, delta + FARW, delta)
        here = jnp.logical_and(d + delta >= 0, d + delta < n_dev)
        live = jnp.logical_and(s < far_count[l], here)
        return jnp.clip(jnp.where(live, pos * LPD + (leaf & (LPD - 1)), 4 * LPD), 0, 4 * LPD)

    copies[3].wait()
    for l in range(LPD):
        copies[4 + l].wait()
        field = far_sums(coupling, l, table, entry) + from_cluster[l * RANK : (l + 1) * RANK]
        product = jnp.dot(
            parts_of(jnp.transpose(field)[:8]), bases[l], preferred_element_type=F32
        )
        product = product[:8] + product[8:16] + product[16:24]
        at = slice(l * LEAF, (l + 1) * LEAF)
        base[:, at] = near[:, at] + product[:NVEC]
    copies[4 + LPD].wait()


def down_kernel(
    far_leaf, far_count, base, down_high, down_low, bases, coupling, top_coupling, second, out,
    table
):
    g = lax.axis_index("grp")
    d = lax.axis_index("dev")
    n_dev = lax.axis_size("dev")
    n_grp = second.shape[0]
    me = g * n_dev + d

    sums = no_sums()
    for h in range(n_grp):
        c = tiles(top_coupling[0, h])
        x = second[(h - GRP_TURN) % n_grp, :, RANK : 2 * RANK]
        x = jnp.where(h != g, x, 0.0)
        for v in range(NVEC):
            sums[v] = sums[v] + c * spread(x, v)[None]
    parts = parts_of(jnp.transpose(lanes_to_matrix(sums))[:8])
    field = rows_by_rows(parts, down_high[...])
    field = field[:8] + field[8:16] + field[16:24] + rows_by_rows(parts[:16], down_low[...])[:8]

    side = (g + jnp.where(d < FARW, -1, 1) - GRP_TURN) & (n_grp - 1)
    for k in range(2):
        start = 2 * RANK + k * WIDE
        fill(table, k * LPD, second[side, :, start : start + WIDE])
    table[2 * LPD] = jnp.zeros((NVEC, 8, RANK), F32)

    def entry(l, s):
        leaf = far_leaf[l, s]
        delta = (leaf >> 2) - me
        which = jnp.where(delta < 0, delta + FARW, delta) & 1
        there = jnp.logical_or(d + delta < 0, d + delta >= n_dev)
        live = jnp.logical_and(s < far_count[l], there)
        return jnp.where(live, which * LPD + (leaf & (LPD - 1)), 2 * LPD)

    for l in range(LPD):
        extra = jnp.transpose(far_sums(coupling, l, table, entry))[:8]
        parts = parts_of(field[:, l * RANK : (l + 1) * RANK] + extra)
        far = jnp.dot(parts, bases[l], preferred_element_type=F32)
        far = far[:8] + far[8:16] + far[16:24]
        at = slice(l * LEAF, (l + 1) * LEAF)
        out[:, at] = base[:, at] + far[:NVEC]


def permute(value, pairs):
    return lax.ppermute(value, ("grp", "dev"), pairs)


def swapped(value, start, count):
    pairs = [(i, (i + 1) % count) for i in range(start, count, 2)]
    return lax.ppermute(value, ("grp", "dev"), pairs + [(j, i) for i, j in pairs])


def in_hbm(*arrays):
    return [pltpu.with_memory_space_constraint(a, pltpu.HBM) for a in arrays]


def params(mib):
    return pltpu.CompilerParams(vmem_limit_bytes=mib * 1024 * 1024)


def cost(flops, size):
    return pl.CostEstimate(flops=flops, bytes_accessed=size, transcendentals=0)


def per_device(
    sources,
    self_near_block,
    neighbour_near_block,
    near_list,
    bases,
    far_leaf,
    far_count,
    leaf_coupling,
    leaf_transfer,
    far_cluster,
    cluster_coupling,
    cluster_transfer,
    top_coupling,
):
    n_dev = lax.axis_size("dev")
    n_grp = lax.axis_size("grp")
    n_all = n_dev * n_grp
    sds = jax.ShapeDtypeStruct
    send = pl.pallas_call(
        up_kernel,
        out_shape=sds((n_dev, NVEC, 2 * RANK + WIDE), F32),
        in_specs=[HBM] * 4,
        out_specs=VMEM,
        scratch_shapes=[
            pltpu.VMEM(sources.shape, BF16),
            pltpu.VMEM(bases.shape, BF16),
            pltpu.VMEM(leaf_transfer.shape, F32),
            pltpu.VMEM(cluster_transfer.shape, F32),
            pltpu.SemaphoreType.DMA((4,)),
        ],
        compiler_params=params(8),
        name="up",
    )(*in_hbm(sources, bases, leaf_transfer, cluster_transfer))
    turned = [(i + TURN) % n_dev for i in range(n_dev)]
    first = lax.all_to_all(send, "dev", 0, 0, axis_index_groups=[turned])
    send, tied = lax.optimization_barrier((send, sources))
    even_swap = swapped(tied, 1, n_all)
    odd_swap = swapped(tied, 0, n_all)
    own, other_v = pl.pallas_call(
        own_kernel,
        out_shape=[sds(sources.shape, F32), sds(neighbour_near_block.shape, BF16)],
        in_specs=[VMEM] + [HBM] * 2,
        out_specs=[VMEM] * 2,
        scratch_shapes=[
            pltpu.VMEM(self_near_block.shape, BF16),
            pltpu.SemaphoreType.DMA((1 + LPD,)),
        ],
        compiler_params=params(8),
        cost_estimate=cost(20000000, 4000000),
        name="own",
    )(*in_hbm(tied, self_near_block, neighbour_near_block))
    near = pl.pallas_call(
        near_kernel,
        out_shape=sds(sources.shape, F32),
        in_specs=[SMEM] + [VMEM] * 5,
        out_specs=VMEM,
        compiler_params=params(4),
        cost_estimate=cost(20000000, 2000000),
        name="near",
    )(*in_hbm(near_list, tied), even_swap, odd_swap, own, other_v)
    first, near = lax.optimization_barrier((first, near))
    send = pl.pallas_call(
        group_kernel,
        out_shape=sds((n_grp, NVEC, 2 * RANK + 2 * WIDE), F32),
        in_specs=[VMEM],
        out_specs=VMEM,
        compiler_params=params(4),
        name="group",
    )(first)
    turned = [(i + GRP_TURN) % n_grp for i in range(n_grp)]
    second = lax.all_to_all(send, "grp", 0, 0, axis_index_groups=[turned])
    base, down_high, down_low, bases_v, coupling_v, top_v = pl.pallas_call(
        mid_kernel,
        out_shape=[
            sds(sources.shape, F32),
            sds((WIDE, RANK), BF16),
            sds((WIDE, RANK), BF16),
            sds(bases.shape, BF16),
            sds(leaf_coupling.shape, F32),
            sds(top_coupling.shape, F32),
        ],
        in_specs=[SMEM] * 3 + [VMEM] * 2 + [HBM] * 6,
        out_specs=[VMEM] * 6,
        scratch_shapes=[
            pltpu.VMEM(leaf_transfer.shape, F32),
            pltpu.VMEM(cluster_transfer.shape, F32),
            pltpu.VMEM(cluster_coupling.shape, F32),
            pltpu.VMEM((4 * LPD + 1, NVEC, 8, RANK), F32),
            pltpu.SemaphoreType.DMA((5 + LPD,)),
        ],
        compiler_params=params(12),
        cost_estimate=cost(40000000, 5000000),
        name="mid",
    )(
        *in_hbm(far_leaf, far_count, far_cluster),
        first,
        near,
        *in_hbm(
            leaf_transfer, cluster_transfer, bases, leaf_coupling, cluster_coupling, top_coupling
        ),
    )
    return pl.pallas_call(
        down_kernel,
        out_shape=sds(sources.shape, F32),
        in_specs=[SMEM] * 2 + [VMEM] * 7,
        out_specs=VMEM,
        scratch_shapes=[
            pltpu.VMEM((2 * LPD + 1, NVEC, 8, RANK), F32),
        ],
        compiler_params=params(8),
        name="down",
    )(
        *in_hbm(far_leaf, far_count),
        base,
        down_high,
        down_low,
        bases_v,
        coupling_v,
        top_v,
        second,
    )


def solution(mesh):
    placed = (
        P(None, ("grp", "dev")),
        P(("grp", "dev"), None, None),
        P(("grp", "dev"), None, None),
        P(("grp", "dev")),
        P(("grp", "dev"), None, None),
        P(("grp", "dev"), None),
        P(("grp", "dev")),
        P(("grp", "dev"), None, None, None),
        P(("grp", "dev"), None, None),
        P(("grp", "dev"), None),
        P(("grp", "dev"), None, None, None),
        P(("grp", "dev"), None, None),
        P("grp", None, None, None),
    )
    return jax.shard_map(
        per_device, mesh=mesh, in_specs=placed, out_specs=P(None, ("grp", "dev")), check_vma=False
    )
```

```python
import jax
import jax.numpy as jnp
from jax import lax
from jax.experimental import pallas as pl
from jax.experimental.pallas import tpu as pltpu
from jax.sharding import PartitionSpec as P

HIGH = lax.Precision.HIGHEST
F32 = jnp.float32
BF16 = jnp.bfloat16
LEAF = 512
RANK = 64
NVEC = 4
LPD = 4
FARW = 3
GRP_TURN = 3
TURN = 15
WIDE = LPD * RANK
VMEM = pl.BlockSpec(memory_space=pltpu.VMEM)
HBM = pl.BlockSpec(memory_space=pltpu.HBM)
SMEM = pl.BlockSpec(memory_space=pltpu.SMEM)


def rows_by_rows(a, b, precision=None):
    return lax.dot_general(
        a, b, (((1,), (1,)), ((), ())), precision=precision, preferred_element_type=F32
    )


def split_dot(a, b):
    a_high, a_low = two_parts(a)
    b_high, b_low = two_parts(b)
    return (
        jnp.dot(a_high, b_high, preferred_element_type=F32)
        + jnp.dot(a_high, b_low, preferred_element_type=F32)
        + jnp.dot(a_low, b_high, preferred_element_type=F32)
    )


def parts_of(rows):
    high = rows.astype(BF16).astype(F32)
    middle = (rows - high).astype(BF16).astype(F32)
    low = rows - high - middle
    return jnp.concatenate([high, middle, low, jnp.zeros_like(low)], axis=0).astype(BF16)


def two_parts(matrix):
    high = matrix.astype(BF16)
    return high, (matrix - high.astype(F32)).astype(BF16)


def close_dot(rows, matrix):
    parts = parts_of(rows)
    out = jnp.dot(parts, matrix[0], preferred_element_type=F32)
    small = jnp.dot(parts[:16], matrix[1], preferred_element_type=F32)
    return out[:8] + (out[8:16] + small[:8]) + (out[16:24] + small[8:16])


def tiles(matrix):
    return matrix.reshape(RANK // 8, 8, RANK)


def no_sums():
    return [jnp.zeros((RANK // 8, 8, RANK), F32) for _ in range(NVEC)]


def lanes_to_matrix(sums):
    lane = lax.broadcasted_iota(jnp.int32, (RANK, 128), 1)
    out = jnp.zeros((RANK, 128), F32)
    for v, s in enumerate(sums):
        column = jnp.sum(s, axis=-1, keepdims=True).reshape(RANK, 1)
        out = jnp.where(lane == v, column, out)
    return out


def spread(rows, v):
    return jnp.broadcast_to(rows[v : v + 1], (8, RANK))


def up_kernel(
    src_h, bases_h, leaf_h, cluster_h, send, src, bases, leaf, cluster, sem
):
    copies = [
        pltpu.make_async_copy(a, b, sem.at[i])
        for i, (a, b) in enumerate(
            (
                (src_h, src),
                (leaf_h, leaf),
                (cluster_h, cluster),
                *((bases_h.at[l], bases.at[l]) for l in range(LPD)),
            )
        )
    ]
    for c in copies:
        c.start()
    copies[0].wait()
    copies[1].wait()
    to_cluster = two_parts(leaf[...].reshape(WIDE, RANK))
    copies[2].wait()
    to_group = two_parts(cluster[0])
    every = []
    for l in range(LPD):
        copies[3 + l].wait()
        every.append(rows_by_rows(src[:, l * LEAF : (l + 1) * LEAF], bases[l]))
    every = jnp.concatenate(every, axis=1)
    cluster_rows = close_dot(jnp.concatenate([every, jnp.zeros_like(every)], axis=0), to_cluster)
    group_rows = close_dot(cluster_rows, to_group)
    row = jnp.concatenate([cluster_rows[:NVEC], group_rows[:NVEC], every], axis=1)
    for i in range(send.shape[0]):
        send[i] = row


def own_kernel(src, self_h, other_h, own, other, block, sem):
    copies = [
        pltpu.make_async_copy(self_h.at[l], block.at[l], sem.at[l]) for l in range(LPD)
    ] + [pltpu.make_async_copy(other_h, other, sem.at[LPD])]
    for c in copies:
        c.start()
    for l in range(LPD):
        at = slice(l * LEAF, (l + 1) * LEAF)
        copies[l].wait()
        own[:, at] = rows_by_rows(src[:, at], block[l])
    copies[LPD].wait()


def near_kernel(near_list, src, even_swap, odd_swap, own, other, near):
    me = lax.axis_index("grp") * lax.axis_size("dev") + lax.axis_index("dev")
    is_odd = (me & 1) == 1
    for l in range(LPD):
        here = jnp.clip(near_list[l] - me * LPD + LPD, 0, 3 * LPD - 1)
        at = pl.multiple_of((here & (LPD - 1)) * LEAF, LEAF)
        which = here >> 2
        x1 = src[:, pl.ds(at, LEAF)]
        x2 = odd_swap[:, pl.ds(at, LEAF)]
        x3 = even_swap[:, pl.ds(at, LEAF)]
        x = jnp.where(which == 1, x1, jnp.where((which == 0) == is_odd, x2, x3))
        at = slice(l * LEAF, (l + 1) * LEAF)
        near[:, at] = own[:, at] + rows_by_rows(x, other[l])


def group_kernel(first, send):
    d = lax.axis_index("dev")
    n_dev = first.shape[0]
    total = jnp.sum(first[:, :, : 2 * RANK], axis=0)
    low = d < FARW
    a = jnp.where(low, jnp.minimum(n_dev - FARW + d, n_dev - 1), jnp.maximum(d - (n_dev - 2), 0))
    b = jnp.where(
        low, jnp.minimum(n_dev - FARW + 1 + d, n_dev - 1), jnp.maximum(d - (n_dev - FARW), 0)
    )
    a, b = (a - TURN) & (n_dev - 1), (b - TURN) & (n_dev - 1)
    row = jnp.concatenate([total, first[a, :, 2 * RANK :], first[b, :, 2 * RANK :]], axis=1)
    for i in range(send.shape[0]):
        send[i] = row


def far_sums(coupling, l, table, entry):
    sums = no_sums()
    for s in range(coupling.shape[1]):
        c = tiles(coupling[l, s])
        at = entry(l, s)
        for v in range(NVEC):
            sums[v] = sums[v] + c * table[at, v][None]
    return lanes_to_matrix(sums)


def fill(table, first_entry, value):
    for l in range(LPD):
        for v in range(NVEC):
            table[first_entry + l, v] = spread(value[:, l * RANK : (l + 1) * RANK], v)


def mid_kernel(
    far_leaf, far_count, far_cluster, first, near, leaf_h, transfer_h, bases_h, coupling_h,
    cluster_h, top_h, base, down_high, down_low, bases, coupling, top_out, leaf_transfer, transfer,
    cluster, table, sem
):
    copies = []
    for a, b in (
        [(leaf_h, leaf_transfer), (transfer_h, transfer), (cluster_h, cluster)]
        + [(bases_h, bases)]
        + [(coupling_h.at[l], coupling.at[l]) for l in range(LPD)]
        + [(top_h, top_out)]
    ):
        copy = pltpu.make_async_copy(a, b, sem.at[len(copies)])
        copy.start()
        copies.append(copy)
    d = lax.axis_index("dev")
    n_dev = lax.axis_size("dev")
    me = lax.axis_index("grp") * n_dev + d

    for pos, off in enumerate((-3, -2, 2, 3)):
        fill(table, pos * LPD, first[(d + off - TURN) & (n_dev - 1), :, 2 * RANK :])
    table[4 * LPD] = jnp.zeros((NVEC, 8, RANK), F32)

    for c in copies[:3]:
        c.wait()
    to_cluster = leaf_transfer[...].reshape(WIDE, RANK)
    to_group = split_dot(to_cluster, transfer[0])
    high = to_group.astype(BF16)
    down_high[...] = high
    down_low[...] = (to_group - high.astype(F32)).astype(BF16)
    sums = no_sums()
    for s in range(far_cluster.shape[1]):
        c = tiles(cluster[0, s])
        x = first[(far_cluster[0, s] - TURN) & (n_dev - 1), :, :RANK]
        for v in range(NVEC):
            sums[v] = sums[v] + c * spread(x, v)[None]
    from_cluster = split_dot(to_cluster, lanes_to_matrix(sums))

    def entry(l, s):
        leaf = far_leaf[l, s]
        delta = (leaf >> 2) - me
        pos = jnp.where(delta < 0, delta + FARW, delta)
        here = jnp.logical_and(d + delta >= 0, d + delta < n_dev)
        live = jnp.logical_and(s < far_count[l], here)
        return jnp.clip(jnp.where(live, pos * LPD + (leaf & (LPD - 1)), 4 * LPD), 0, 4 * LPD)

    copies[3].wait()
    for l in range(LPD):
        copies[4 + l].wait()
        field = far_sums(coupling, l, table, entry) + from_cluster[l * RANK : (l + 1) * RANK]
        product = jnp.dot(
            parts_of(jnp.transpose(field)[:8]), bases[l], preferred_element_type=F32
        )
        product = product[:8] + product[8:16] + product[16:24]
        at = slice(l * LEAF, (l + 1) * LEAF)
        base[:, at] = near[:, at] + product[:NVEC]
    copies[4 + LPD].wait()


def down_kernel(
    far_leaf, far_count, base, down_high, down_low, bases, coupling, top_coupling, second, out,
    table
):
    g = lax.axis_index("grp")
    d = lax.axis_index("dev")
    n_dev = lax.axis_size("dev")
    n_grp = second.shape[0]
    me = g * n_dev + d

    sums = no_sums()
    for h in range(n_grp):
        c = tiles(top_coupling[0, h])
        x = second[(h - GRP_TURN) % n_grp, :, RANK : 2 * RANK]
        x = jnp.where(h != g, x, 0.0)
        for v in range(NVEC):
            sums[v] = sums[v] + c * spread(x, v)[None]
    parts = parts_of(jnp.transpose(lanes_to_matrix(sums))[:8])
    field = rows_by_rows(parts, down_high[...])
    field = field[:8] + field[8:16] + field[16:24] + rows_by_rows(parts[:16], down_low[...])[:8]

    side = (g + jnp.where(d < FARW, -1, 1) - GRP_TURN) & (n_grp - 1)
    for k in range(2):
        start = 2 * RANK + k * WIDE
        fill(table, k * LPD, second[side, :, start : start + WIDE])
    table[2 * LPD] = jnp.zeros((NVEC, 8, RANK), F32)

    def entry(l, s):
        leaf = far_leaf[l, s]
        delta = (leaf >> 2) - me
        which = jnp.where(delta < 0, delta + FARW, delta) & 1
        there = jnp.logical_or(d + delta < 0, d + delta >= n_dev)
        live = jnp.logical_and(s < far_count[l], there)
        return jnp.where(live, which * LPD + (leaf & (LPD - 1)), 2 * LPD)

    for l in range(LPD):
        extra = jnp.transpose(far_sums(coupling, l, table, entry))[:8]
        parts = parts_of(field[:, l * RANK : (l + 1) * RANK] + extra)
        far = jnp.dot(parts, bases[l], preferred_element_type=F32)
        far = far[:8] + far[8:16] + far[16:24]
        at = slice(l * LEAF, (l + 1) * LEAF)
        out[:, at] = base[:, at] + far[:NVEC]


def permute(value, pairs):
    return lax.ppermute(value, ("grp", "dev"), pairs)


def swapped(value, start, count):
    pairs = [(i, (i + 1) % count) for i in range(start, count, 2)]
    return lax.ppermute(value, ("grp", "dev"), pairs + [(j, i) for i, j in pairs])


def in_hbm(*arrays):
    return [pltpu.with_memory_space_constraint(a, pltpu.HBM) for a in arrays]


def params(mib):
    return pltpu.CompilerParams(vmem_limit_bytes=mib * 1024 * 1024)


def cost(flops, size):
    return pl.CostEstimate(flops=flops, bytes_accessed=size, transcendentals=0)


def per_device(
    sources,
    self_near_block,
    neighbour_near_block,
    near_list,
    bases,
    far_leaf,
    far_count,
    leaf_coupling,
    leaf_transfer,
    far_cluster,
    cluster_coupling,
    cluster_transfer,
    top_coupling,
):
    n_dev = lax.axis_size("dev")
    n_grp = lax.axis_size("grp")
    n_all = n_dev * n_grp
    sds = jax.ShapeDtypeStruct
    send = pl.pallas_call(
        up_kernel,
        out_shape=sds((n_dev, NVEC, 2 * RANK + WIDE), F32),
        in_specs=[HBM] * 4,
        out_specs=VMEM,
        scratch_shapes=[
            pltpu.VMEM(sources.shape, BF16),
            pltpu.VMEM(bases.shape, BF16),
            pltpu.VMEM(leaf_transfer.shape, F32),
            pltpu.VMEM(cluster_transfer.shape, F32),
            pltpu.SemaphoreType.DMA((3 + LPD,)),
        ],
        compiler_params=params(8),
        name="up",
    )(*in_hbm(sources, bases, leaf_transfer, cluster_transfer))
    turned = [(i + TURN) % n_dev for i in range(n_dev)]
    first = lax.all_to_all(send, "dev", 0, 0, axis_index_groups=[turned])
    send, tied = lax.optimization_barrier((send, sources))
    even_swap = swapped(tied, 1, n_all)
    odd_swap = swapped(tied, 0, n_all)
    own, other_v = pl.pallas_call(
        own_kernel,
        out_shape=[sds(sources.shape, F32), sds(neighbour_near_block.shape, BF16)],
        in_specs=[VMEM] + [HBM] * 2,
        out_specs=[VMEM] * 2,
        scratch_shapes=[
            pltpu.VMEM(self_near_block.shape, BF16),
            pltpu.SemaphoreType.DMA((1 + LPD,)),
        ],
        compiler_params=params(8),
        cost_estimate=cost(20000000, 4000000),
        name="own",
    )(*in_hbm(tied, self_near_block, neighbour_near_block))
    near = pl.pallas_call(
        near_kernel,
        out_shape=sds(sources.shape, F32),
        in_specs=[SMEM] + [VMEM] * 5,
        out_specs=VMEM,
        compiler_params=params(4),
        cost_estimate=cost(20000000, 2000000),
        name="near",
    )(*in_hbm(near_list, tied), even_swap, odd_swap, own, other_v)
    first, near = lax.optimization_barrier((first, near))
    send = pl.pallas_call(
        group_kernel,
        out_shape=sds((n_grp, NVEC, 2 * RANK + 2 * WIDE), F32),
        in_specs=[VMEM],
        out_specs=VMEM,
        compiler_params=params(4),
        name="group",
    )(first)
    turned = [(i + GRP_TURN) % n_grp for i in range(n_grp)]
    second = lax.all_to_all(send, "grp", 0, 0, axis_index_groups=[turned])
    base, down_high, down_low, bases_v, coupling_v, top_v = pl.pallas_call(
        mid_kernel,
        out_shape=[
            sds(sources.shape, F32),
            sds((WIDE, RANK), BF16),
            sds((WIDE, RANK), BF16),
            sds(bases.shape, BF16),
            sds(leaf_coupling.shape, F32),
            sds(top_coupling.shape, F32),
        ],
        in_specs=[SMEM] * 3 + [VMEM] * 2 + [HBM] * 6,
        out_specs=[VMEM] * 6,
        scratch_shapes=[
            pltpu.VMEM(leaf_transfer.shape, F32),
            pltpu.VMEM(cluster_transfer.shape, F32),
            pltpu.VMEM(cluster_coupling.shape, F32),
            pltpu.VMEM((4 * LPD + 1, NVEC, 8, RANK), F32),
            pltpu.SemaphoreType.DMA((5 + LPD,)),
        ],
        compiler_params=params(12),
        cost_estimate=cost(40000000, 5000000),
        name="mid",
    )(
        *in_hbm(far_leaf, far_count, far_cluster),
        first,
        near,
        *in_hbm(
            leaf_transfer, cluster_transfer, bases, leaf_coupling, cluster_coupling, top_coupling
        ),
    )
    return pl.pallas_call(
        down_kernel,
        out_shape=sds(sources.shape, F32),
        in_specs=[SMEM] * 2 + [VMEM] * 7,
        out_specs=VMEM,
        scratch_shapes=[
            pltpu.VMEM((2 * LPD + 1, NVEC, 8, RANK), F32),
        ],
        compiler_params=params(8),
        name="down",
    )(
        *in_hbm(far_leaf, far_count),
        base,
        down_high,
        down_low,
        bases_v,
        coupling_v,
        top_v,
        second,
    )


def solution(mesh):
    placed = (
        P(None, ("grp", "dev")),
        P(("grp", "dev"), None, None),
        P(("grp", "dev"), None, None),
        P(("grp", "dev")),
        P(("grp", "dev"), None, None),
        P(("grp", "dev"), None),
        P(("grp", "dev")),
        P(("grp", "dev"), None, None, None),
        P(("grp", "dev"), None, None),
        P(("grp", "dev"), None),
        P(("grp", "dev"), None, None, None),
        P(("grp", "dev"), None, None),
        P("grp", None, None, None),
    )
    return jax.shard_map(
        per_device, mesh=mesh, in_specs=placed, out_specs=P(None, ("grp", "dev")), check_vma=False
    )
```
